32 devices in a mesh: band: 8 (over z, y), grid: 4 (over x, core).
Axes of the slice: x: 2, y: 2, z: 4, core: 2. Of those that a mesh axis runs over, the one named last changes fastest.
Arguments:
- orbitals: bfloat16 [32, 96, 9216], P('band', 'grid'), may hold values from -6 to 6
- kernel: float32 [96, 9216], P('grid'), may hold values from 0.02 to 1
Outputs:
- update: float32 [32, 96, 9216], P('band', 'grid')
The draws below stay inside these ranges and needn't reach their ends.
All inputs are finite; a program needn't handle non-finite values.
Results may differ from the reference program's by a relative error of at most 0.0049.
Values may be sent and summed in bfloat16 or wider, within the bound.
No kernel may reach another device: no remote copies, remote signals or barrier semaphores. Data moves between devices by JAX's collectives and lax.ppermute only.
A program may use at most 128 MiB of HBM per device.

```python
import math
import jax
import jax.numpy as jnp
from jax import lax

GRID_N = 96
BLOCK_BANDS = 4
DIST = 1
BANDS = 32
N_BAND = 8


def block_scale(key, dims, cuts, low, top_value):
    gain = 1.0
    for position, parts in cuts:
        steps = jax.random.uniform(jax.random.fold_in(jax.random.fold_in(key, 6), position), (parts,), jnp.float32, low / len(cuts), top_value / len(cuts))
        gain = gain * jnp.repeat(jnp.exp(steps), dims[position] // parts).reshape((-1,) + (1,) * (len(dims) - 1 - position))
    return gain


def noise(key, shape, spread, reach, split=(), held_as=jnp.bfloat16):
    level = block_scale(key, shape, split, -0.22, 0.18) if split else 1.0
    result = jax.random.normal(key, shape, jnp.float32) * spread * level
    return jnp.minimum(jnp.maximum(result, -reach), reach).astype(held_as)


def setup_inputs(seed: int = 0) -> dict:
    key_list = jax.random.split(jax.random.key(seed), 3)
    return {
        "orbitals": noise(key_list[0], (BANDS, GRID_N, GRID_N * GRID_N), 1.0, 6.0, ((0, 8), (1, 4))),
        "kernel": jnp.clip(jnp.exp(math.log(1.0) - 3.912023 * jax.random.uniform(key_list[1], (GRID_N, GRID_N * GRID_N), jnp.float32) ** block_scale(key_list[1], (GRID_N, GRID_N * GRID_N), ((0, 4),), -0.2, 0.2)), 0.02, 1.0),
    }


def make_tables(count):
    indices = jnp.arange(count, dtype=jnp.int32)
    angles = ((indices[:, None] * indices[None, :]) % count).astype(jnp.float32) * (2.0 * math.pi / count)
    cosine = jnp.cos(angles).astype(jnp.bfloat16)
    sine = jnp.sin(angles).astype(jnp.bfloat16)
    real_table = jnp.stack([cosine, -sine])
    forward = jnp.stack([jnp.stack([cosine, sine]), jnp.stack([-sine, cosine])])
    backward = jnp.stack([jnp.stack([cosine, -sine]), jnp.stack([sine, cosine])])
    return real_table, forward, backward


def wide(array):
    return array.astype(jnp.float32)


def potentials(density, scaled, real_table, forward, backward):
    along_z = jnp.einsum('ckz,xyzp->xykcp', wide(real_table), wide(density)).astype(jnp.bfloat16)
    along_zy = jnp.einsum('dcjy,xykcp->xjkdp', wide(forward), wide(along_z)).astype(jnp.bfloat16)
    summed = jnp.einsum('dcgx,xjkcp->gjkdp', wide(forward), wide(along_zy))
    spectrum = (summed * scaled[:, :, :, None, None]).astype(jnp.bfloat16)
    back_x = jnp.einsum('dcxg,gjkcp->xjkdp', wide(backward), wide(spectrum)).astype(jnp.bfloat16)
    back_xy = jnp.einsum('dcyj,xjkcp->xykdp', wide(backward), wide(back_x)).astype(jnp.bfloat16)
    return jnp.einsum('ckz,xykcp->xyzp', wide(real_table), wide(back_xy))


def reference(orbitals, kernel):
    count = GRID_N
    tables = make_tables(count)
    scaled = kernel.reshape(count, count, count).transpose(1, 0, 2) / (count ** 3)
    blocks = orbitals.reshape(N_BAND, BLOCK_BANDS, count, count, count)
    partners = jnp.roll(blocks, DIST, axis=0)

    def one_block(operands):
        own_block, other_block = operands
        own_last = own_block.transpose(1, 2, 3, 0)
        other_last = other_block.transpose(1, 2, 3, 0)
        density = (wide(own_last)[..., :, None] * wide(other_last)[..., None, :]).astype(jnp.bfloat16)
        density = density.reshape(count, count, count, BLOCK_BANDS * BLOCK_BANDS)
        potential = potentials(density, scaled, *tables).reshape(count, count, count, BLOCK_BANDS, BLOCK_BANDS)
        kept = -jnp.einsum('xyzab,xyzb->xyza', potential, wide(other_last))
        sent = -jnp.einsum('xyzab,xyza->xyzb', potential, wide(own_last))
        return kept.transpose(3, 0, 1, 2), sent.transpose(3, 0, 1, 2)

    kept, sent = lax.map(one_block, (blocks, partners))
    update = kept + jnp.roll(sent, -DIST, axis=0)
    return update.reshape(BANDS, count, count * count)
```

```python
import functools

import jax
import jax.numpy as jnp
import ml_dtypes
import numpy as np
from jax import lax
from jax.experimental import pallas as pl
from jax.experimental.pallas import tpu as pltpu
from jax.sharding import PartitionSpec as P

DIST = 1
LANES = 128
TILES = 3
GROUPS = 3
UNROLL = 8
BF = jnp.bfloat16
F32 = jnp.float32
VMEM_BYTES = 60 * 1024 * 1024


def dot(a, b):
    return jnp.dot(a, b, preferred_element_type=F32)


def half(a):
    return np.asarray(a, np.float32).astype(ml_dtypes.bfloat16)


def complex_tables(count):
    j = np.arange(count)
    angles = (j[:, None] * j[None, :] % count).astype(np.float32) * np.float32(2.0 * np.pi / count)
    cosine = half(np.cos(angles)).astype(np.float32)
    sine = half(np.sin(angles)).astype(np.float32)
    forward = np.block([[cosine, sine], [-sine, cosine]])
    backward = np.block([[cosine, -sine], [sine, cosine]])
    return forward, backward


def line_spans(count):
    per = TILES * LANES // count
    lines = [(s * count // LANES, -(-(s + 1) * count // LANES)) for s in range(per)]
    tiles = [(t * LANES // count, -(-(t + 1) * LANES // count)) for t in range(TILES)]
    return lines, tiles


def z_tables(count):
    forward, backward = complex_tables(count)
    lines, tiles = line_spans(count)
    cut, lay = [], []
    for s, (t0, t1) in enumerate(lines):
        w = np.zeros((2, (t1 - t0) * LANES, 2, LANES), np.float32)
        first = s * count - t0 * LANES
        for c in range(2):
            for d in range(2):
                w[c, first:first + count, d, :count] = forward[d * count:(d + 1) * count, c * count:(c + 1) * count].T
        cut.append(half(w.reshape(-1, 2 * LANES)))
    for t, (s0, s1) in enumerate(tiles):
        w = np.zeros((s1 - s0, 2, LANES, 2, LANES), np.float32)
        for s in range(s0, s1):
            for z in range(count):
                lane = s * count + z - t * LANES
                if 0 <= lane < LANES:
                    for c in range(2):
                        for d in range(2):
                            w[s - s0, c, :count, d, lane] = backward[d * count + z, c * count:(c + 1) * count]
        lay.append(half(w.reshape(-1, 2 * LANES)))
    return cut, lay


def piece_planes(count, ga, gb, device):
    rows = count // (ga * gb)
    ai, bi = divmod(device, gb)
    owners = [((ai + s) % ga) * gb + (bi + t) % gb for s in range(ga) for t in range(gb)]
    return np.concatenate([np.arange(o * rows, (o + 1) * rows) for o in owners])


def device_tables(count, ga, gb):
    forward, backward = complex_tables(count)
    near = count // ga
    fwd, bwd, mirror = [], [], []
    for device in range(ga * gb):
        planes = piece_planes(count, ga, gb, device)
        fwd.append(np.concatenate([forward[:, planes], forward[:, count + planes]], axis=1))
        bwd.append(np.concatenate([backward[planes[:near]], backward[count + planes[:near]]], axis=0))
        place = np.eye(count, dtype=np.float32)[:, planes]
        flip = place[(-np.arange(count)) % count]
        mirror.append(np.concatenate([place, flip], axis=1))
    return half(np.stack(fwd)), half(np.stack(bwd)), half(np.stack(mirror))


def line_selectors(count):
    lines, _ = line_spans(count)
    picks = []
    for s, (t0, t1) in enumerate(lines):
        w = np.zeros(((t1 - t0) * LANES, 2, LANES), np.float32)
        for z in range(count):
            w[s * count + z - t0 * LANES, 0, z] = 1
            w[s * count + z - t0 * LANES, 1, (-z) % count] = 1
        picks.append(half(w.reshape(-1, 2 * LANES)))
    return picks


def kernel_body(count, n, *refs):
    pieces, mirror = refs[:n], refs[n]
    lines, _ = line_spans(count)
    picks = refs[n + 1:n + 1 + len(lines)]
    out_ref, cut_ref = refs[n + 1 + len(lines):]
    per = len(lines)
    width = TILES * LANES

    def cut(group, carry):
        lanes = pl.ds(pl.multiple_of(group * width, LANES), width)
        k = jnp.concatenate([r[:, lanes].astype(F32) for r in pieces], axis=0).astype(BF)
        for s, (t0, t1) in enumerate(lines):
            cut_ref[group * per + s] = dot(k[:, t0 * LANES:t1 * LANES], picks[s][...]).astype(BF)
        return carry

    lax.fori_loop(0, count // per, cut, 0)

    def join(step, carry):
        for u in range(4):
            gx = step * 4 + u
            back = lax.rem(count - gx, count)
            both = jnp.concatenate([cut_ref[gx][:, :LANES], cut_ref[back][:, LANES:]], axis=0)
            out_ref[gx] = dot(mirror[...], both) * (0.5 / count**3)
        return carry

    lax.fori_loop(0, count // 4, join, 0)


def whole_kernel(pieces, mirror, count):
    picks = line_selectors(count)
    vmem = pl.BlockSpec(memory_space=pltpu.VMEM)
    ins = [*pieces, mirror, *picks]
    return pl.pallas_call(
        functools.partial(kernel_body, count, len(pieces)),
        out_shape=jax.ShapeDtypeStruct((count, count, LANES), F32),
        in_specs=[vmem] * len(ins),
        out_specs=vmem,
        scratch_shapes=[pltpu.VMEM((count, count, 2 * LANES), BF)],
        compiler_params=pltpu.CompilerParams(vmem_limit_bytes=VMEM_BYTES),
        name="symmetric_kernel",
    )(*ins)


def unit_body(count, n, near, has_prev, *refs):
    refs = list(refs)

    def take(k):
        return [refs.pop(0) for _ in range(k)]

    lines, tiles = line_spans(count)
    per = len(lines)
    width = TILES * LANES
    a_refs, b_refs = take(n), take(n)
    k_ref, x_fwd, x_bwd, y_fwd, y_bwd = take(5)
    cut, lay = take(per), take(TILES)
    prev = take(1)[0] if has_prev else None
    sent_refs, kept_ref = take(near), take(1)[0]
    s_ref, r_ref = take(2)
    ra, rows = a_refs[0].shape[:2]
    planes = near * rows
    steps = count // (per * GROUPS)

    def stack(pieces):
        return jnp.concatenate([p.astype(F32) for p in pieces], axis=0)

    def forward(step, carry):
        rho = [[], []]
        for g in range(GROUPS):
            lanes = pl.ds(pl.multiple_of((step * GROUPS + g) * width, LANES), width)
            b = stack([r[:, lanes] for r in b_refs])
            for k in range(2):
                if k < ra:
                    rho[k].append((stack([r[k, :, lanes] for r in a_refs]) * b).astype(BF))
                else:
                    rho[k].append(jnp.zeros((count, width), BF))
        rho = [jnp.concatenate(r, axis=0) for r in rho]
        along = []
        for s, (t0, t1) in enumerate(lines):
            lhs = jnp.concatenate([r[:, t0 * LANES:t1 * LANES] for r in rho], axis=1)
            along.append(dot(lhs, cut[s][...]).astype(BF))
        for g in range(GROUPS):
            for s in range(0, per, 2):
                pair = []
                for e in range(2):
                    w = along[s + e][g * count:(g + 1) * count]
                    pair.append(jnp.concatenate([w[:, :LANES], w[:, LANES:]], axis=0))
                out = dot(x_fwd[...], jnp.concatenate(pair, axis=1))
                y = (step * GROUPS + g) * per + s
                for e in range(2):
                    s_ref[pl.ds(y + e, 2 * count, count), :] = out[:, e * LANES:(e + 1) * LANES]
        return carry

    lax.fori_loop(0, steps, forward, 0)

    def plane_pair(ref, first, second):
        return jnp.concatenate(
            [
                jnp.concatenate(
                    [ref[pl.ds(pl.multiple_of((c * count + i) * count, 8), count), :].astype(BF) for c in range(2)],
                    axis=0,
                )
                for i in (first, second)
            ],
            axis=1,
        )

    def middle(step, carry):
        firsts = [(step * UNROLL + u) * 2 for u in range(UNROLL)]
        summed = [dot(y_fwd[...], plane_pair(s_ref, gx, gx + 1)) for gx in firsts]
        spectra = []
        for gx, value in zip(firsts, summed):
            scale = jnp.concatenate([k_ref[gx], k_ref[gx + 1]], axis=1)
            spectra.append(
                jnp.concatenate([(value[:count] * scale).astype(BF), (value[count:] * scale).astype(BF)], axis=0)
            )
        backs = [dot(y_bwd[...], spectrum) for spectrum in spectra]
        for gx, value in zip(firsts, backs):
            for e in range(2):
                r_ref[pl.ds(gx + e, 2 * count, count), :] = value[:, e * LANES:(e + 1) * LANES]
        return carry

    lax.fori_loop(0, count // (2 * UNROLL), middle, 0)

    def backward(step, carry):
        columns = []
        for g in range(GROUPS):
            row = []
            for s in range(0, per, 2):
                y = (step * GROUPS + g) * per + s
                out = dot(x_bwd[...], plane_pair(r_ref, y, y + 1)).astype(BF)
                for e in range(2):
                    w = out[:, e * LANES:(e + 1) * LANES]
                    row.append(jnp.concatenate([w[:planes], w[planes:]], axis=1))
            columns.append(row)
        for t, (s0, s1) in enumerate(tiles):
            lhs = jnp.concatenate([jnp.concatenate(row[s0:s1], axis=1) for row in columns], axis=0)
            potential = dot(lhs, lay[t][...])
            for g in range(GROUPS):
                lanes = pl.ds(pl.multiple_of((step * GROUPS + g) * width + t * LANES, LANES), LANES)
                v = potential[g * planes:(g + 1) * planes]
                b = stack([r[:, lanes] for r in b_refs[:near]])
                sent = None
                for k in range(ra):
                    minus = -v[:, k * LANES:(k + 1) * LANES]
                    term = minus * stack([r[k, :, lanes] for r in a_refs[:near]])
                    sent = term if sent is None else sent + term
                    kept = minus * b
                    for p in range(near):
                        piece = kept[p * rows:(p + 1) * rows]
                        if has_prev:
                            piece = piece + prev[p, k, :, lanes]
                        kept_ref[p, k, :, lanes] = piece
                for p in range(near):
                    sent_refs[p][:, lanes] = sent[p * rows:(p + 1) * rows].astype(BF)
        return carry

    lax.fori_loop(0, steps, backward, 0)


def unit(a, b, kern, x_fwd, x_bwd, near, prev):
    count = kern.shape[0]
    n = len(a)
    ra, rows, width = a[0].shape
    y_fwd, y_bwd = (half(t) for t in complex_tables(count))
    cut, lay = z_tables(count)
    ins = [*a, *b, kern, x_fwd, x_bwd, y_fwd, y_bwd, *cut, *lay] + ([] if prev is None else [prev])
    vmem = pl.BlockSpec(memory_space=pltpu.VMEM)
    outs = pl.pallas_call(
        functools.partial(unit_body, count, n, near, prev is not None),
        out_shape=[jax.ShapeDtypeStruct((rows, width), BF)] * near
        + [jax.ShapeDtypeStruct((near, ra, rows, width), F32)],
        in_specs=[vmem] * len(ins),
        out_specs=[vmem] * (near + 1),
        scratch_shapes=[pltpu.VMEM((2 * count * count, LANES), F32)] * 2,
        compiler_params=pltpu.CompilerParams(vmem_limit_bytes=VMEM_BYTES),
        cost_estimate=pl.CostEstimate(flops=10 * 10**9, bytes_accessed=16 * 10**6, transcendentals=0),
        name="pair_potentials",
    )(*ins)
    return outs[:near], outs[near]


def split_of(n):
    gb = 1
    while gb * gb < n and gb < 4:
        gb *= 2
    return n // gb, gb


def local(orbitals, kernel, *, ga, gb):
    band_count, rows, width = orbitals.shape
    n = ga * gb
    count = rows * n
    na = band_count // gb
    blocks = lax.axis_size("band")
    me = lax.axis_index("grid")
    ai, bi = me // gb, me % gb

    def hop(x, distance):
        return lax.ppermute(x, "band", [(i, (i + distance) % blocks) for i in range(blocks)])

    def to_a(x, s):
        return lax.ppermute(x, "grid", [(((i // gb + s) % ga) * gb + i % gb, i) for i in range(n)])

    def to_b(x, t):
        return lax.ppermute(x, "grid", [((i // gb) * gb + (i % gb + t) % gb, i) for i in range(n)])

    def bands_of(core):
        return lax.dynamic_slice_in_dim(orbitals, core * na, na, 0)

    fwd, bwd, mirror = device_tables(count, ga, gb)
    x_fwd, x_bwd, mirror = (lax.dynamic_index_in_dim(jnp.asarray(t), me, 0, False) for t in (fwd, bwd, mirror))

    a = {(0, 0): bands_of(bi)}
    for t in range(1, gb):
        a[0, t] = to_b(bands_of((bi + gb - t) % gb), t)
    hops = [hop(orbitals[j], DIST) for j in range(band_count)]
    for s in range(1, ga):
        for t in range(gb):
            a[s, t] = to_a(a[0, t], s)
    k = {(0, 0): kernel.astype(BF)}
    for s in range(1, ga):
        k[s, 0] = to_a(k[0, 0], s)
    for s in range(ga):
        for t in range(1, gb):
            k[s, t] = to_b(k[s, 0], t)
    order = [(s, t) for s in range(ga) for t in range(gb)]
    kern = whole_kernel([k[o] for o in order], mirror, count)

    kept = None
    returned = []
    for j in range(band_count):
        b = {(0, 0): hops[j]}
        for s in range(1, ga):
            b[s, 0] = to_a(b[0, 0], s)
        for s in range(ga):
            for t in range(1, gb):
                b[s, t] = to_b(b[s, 0], t)
        sent, kept = unit([a[o] for o in order], [b[o] for o in order], kern, x_fwd, x_bwd, gb, kept)
        total = sent[0].astype(F32)
        for t in range(1, gb):
            total = total + to_b(sent[t], gb - t).astype(F32)
        returned.append(hop(total.astype(BF), -DIST))

    shares = [kept[0]] + [to_b(kept[t].astype(BF), gb - t).astype(F32) for t in range(1, gb)]
    blocks_kept = []
    for block in range(gb):
        which = (bi - block + gb) % gb
        value = shares[0]
        for t in range(1, gb):
            value = jnp.where(which == t, shares[t], value)
        blocks_kept.append(value)
    return jnp.concatenate(blocks_kept, axis=0) + jnp.stack(returned).astype(F32)


def solution(mesh):
    ga, gb = split_of(mesh.shape["grid"])
    placed = (P("band", "grid", None), P("grid", None))
    return jax.shard_map(
        functools.partial(local, ga=ga, gb=gb),
        mesh=mesh,
        in_specs=placed,
        out_specs=P("band", "grid", None),
        check_vma=False,
    )
```

```python
import functools

import jax
import jax.numpy as jnp
import ml_dtypes
import numpy as np
from jax import lax
from jax.experimental import pallas as pl
from jax.experimental.pallas import tpu as pltpu
from jax.sharding import PartitionSpec as P

DIST = 1
LANES = 128
TILES = 3
GROUPS = 12
UNROLL = 12
CHUNKS = 2
PITCH = 4
BF = jnp.bfloat16
F32 = jnp.float32
FLOPS = 10**11
VMEM_BYTES = 62 * 1024 * 1024


def dot(a, b):
    return jnp.dot(a, b, preferred_element_type=F32)


def half(a):
    return np.asarray(a, np.float32).astype(ml_dtypes.bfloat16)


def complex_tables(count):
    j = np.arange(count)
    angles = (j[:, None] * j[None, :] % count).astype(np.float32) * np.float32(2.0 * np.pi / count)
    cosine = half(np.cos(angles)).astype(np.float32)
    sine = half(np.sin(angles)).astype(np.float32)
    forward = np.block([[cosine, sine], [-sine, cosine]])
    backward = np.block([[cosine, -sine], [sine, cosine]])
    return forward, backward


def line_spans(count):
    per = TILES * LANES // count
    lines = [(s * count // LANES, -(-(s + 1) * count // LANES)) for s in range(per)]
    tiles = [(t * LANES // count, -(-(t + 1) * LANES // count)) for t in range(TILES)]
    return lines, tiles


def z_tables(count):
    forward, backward = complex_tables(count)
    lines, tiles = line_spans(count)
    cut, lay = [], []
    for s, (t0, t1) in enumerate(lines):
        w = np.zeros((2, (t1 - t0) * LANES, 2, LANES), np.float32)
        first = s * count - t0 * LANES
        for c in range(2):
            for d in range(2):
                w[c, first:first + count, d, :count] = forward[d * count:(d + 1) * count, c * count:(c + 1) * count].T
        cut.append(half(w.reshape(-1, 2 * LANES)))
    for t, (s0, s1) in enumerate(tiles):
        w = np.zeros((s1 - s0, 2, LANES, 2, LANES), np.float32)
        for s in range(s0, s1):
            for z in range(count):
                lane = s * count + z - t * LANES
                if 0 <= lane < LANES:
                    for c in range(2):
                        for d in range(2):
                            w[s - s0, c, :count, d, lane] = backward[d * count + z, c * count:(c + 1) * count]
        lay.append(half(w.reshape(-1, 2 * LANES)))
    return cut, lay


def piece_planes(count, ga, gb, device):
    rows = count // (ga * gb)
    ai, bi = divmod(device, gb)
    owners = [((ai + s) % ga) * gb + (bi + t) % gb for s in range(ga) for t in range(gb)]
    return np.concatenate([np.arange(o * rows, (o + 1) * rows) for o in owners])


def device_tables(count, ga, gb):
    forward, backward = complex_tables(count)
    near = count // ga
    fwd, bwd, mirror = [], [], []
    for device in range(ga * gb):
        planes = piece_planes(count, ga, gb, device)
        fwd.append(np.concatenate([forward[:, planes], forward[:, count + planes]], axis=1))
        bwd.append(np.concatenate([backward[planes[:near]], backward[count + planes[:near]]], axis=0))
        place = np.eye(count, dtype=np.float32)[:, planes]
        flip = place[(-np.arange(count)) % count]
        mirror.append(np.concatenate([place, flip], axis=1))
    return half(np.stack(fwd)), half(np.stack(bwd)), half(np.stack(mirror))


def line_selectors(count):
    lines, _ = line_spans(count)
    picks = []
    for s, (t0, t1) in enumerate(lines):
        w = np.zeros(((t1 - t0) * LANES, 2, LANES), np.float32)
        for z in range(count):
            w[s * count + z - t0 * LANES, 0, z] = 1
            w[s * count + z - t0 * LANES, 1, (-z) % count] = 1
        picks.append(half(w.reshape(-1, 2 * LANES)))
    return picks


def kernel_body(count, n, *refs):
    pieces, mirror = refs[:n], refs[n]
    lines, _ = line_spans(count)
    picks = refs[n + 1:n + 1 + len(lines)]
    out_ref, cut_ref = refs[n + 1 + len(lines):]
    per = len(lines)
    width = TILES * LANES
    unrolled = 6

    def cut(step, carry):
        for u in range(unrolled):
            group = step * unrolled + u
            lanes = pl.ds(pl.multiple_of(group * width, LANES), width)
            k = jnp.concatenate([r[:, lanes].astype(F32) for r in pieces], axis=0).astype(BF)
            for s, (t0, t1) in enumerate(lines):
                cut_ref[group * per + s] = dot(k[:, t0 * LANES:t1 * LANES], picks[s][...]).astype(BF)
        return carry

    lax.fori_loop(0, count // (per * unrolled), cut, 0)

    def join(step, carry):
        for u in range(0, 16, 2):
            both = []
            for e in range(2):
                gx = step * 16 + u + e
                back = lax.rem(count - gx, count)
                both.append(jnp.concatenate([cut_ref[gx][:, :LANES], cut_ref[back][:, LANES:]], axis=0))
            value = dot(mirror[...], jnp.concatenate(both, axis=1)) * (0.5 / count**3)
            for e in range(2):
                out_ref[step * 16 + u + e] = value[:, e * LANES:(e + 1) * LANES]
        return carry

    lax.fori_loop(0, count // 16, join, 0)


def whole_kernel(pieces, mirror, count):
    picks = line_selectors(count)
    vmem = pl.BlockSpec(memory_space=pltpu.VMEM)
    ins = [*pieces, mirror, *picks]
    return pl.pallas_call(
        functools.partial(kernel_body, count, len(pieces)),
        out_shape=jax.ShapeDtypeStruct((count, count, LANES), F32),
        in_specs=[vmem] * len(ins),
        out_specs=vmem,
        scratch_shapes=[pltpu.VMEM((count, count, 2 * LANES), BF)],
        compiler_params=pltpu.CompilerParams(vmem_limit_bytes=VMEM_BYTES),
        cost_estimate=pl.CostEstimate(flops=FLOPS, bytes_accessed=10**3, transcendentals=0),
        name="symmetric_kernel",
    )(*ins)


def unit_body(count, n, near, a_count, b_count, places, kept_held, core_ref, *refs):
    refs = list(refs)

    def take(k):
        return [refs.pop(0) for _ in range(k)]

    lines, tiles = line_spans(count)
    per = len(lines)
    width = TILES * LANES
    pieces = take((a_count + b_count) * n)
    kern, x_tables, y_tables, z_tables_ref = take(4)
    kept_in = [take(near) for _ in range(a_count)] if kept_held else None
    sent_out, kept_out = take(b_count * near), take(a_count * near)
    held, k_ref, x_ref, y_ref, z_ref, sent_near, sent_rest, kept_ref, s_ref, r_ref = take(10)
    in_sem, table_sem, kept_sem, sent_sem, out_sem = take(5)
    rows = pieces[0].shape[1]
    where = [core_ref[0] * step + offset if step else offset for step, offset in places]
    pitch = count + PITCH
    planes = near * rows
    steps = count // (per * GROUPS)
    chunk = count * count // CHUNKS
    pairs = [(i, j) for i in range(a_count) for j in range(b_count)]

    def lanes_of(part):
        return slice(part * chunk, (part + 1) * chunk)

    def piece_in(step, p):
        return pltpu.make_async_copy(
            pieces[p].at[where[p], :, lanes_of(step)], held.at[p, :, lanes_of(step)], in_sem.at[step, p]
        )

    def outgoing(step):
        lanes = lanes_of(step)
        copies = []
        for j in range(b_count):
            for p in range(near):
                source = sent_rest.at[j, p - 1, :, lanes] if p else sent_near.at[j, :, lanes]
                copies.append(
                    pltpu.make_async_copy(source, sent_out[j * near + p].at[:, lanes], sent_sem.at[step, j * near + p])
                )
        for i in range(a_count):
            for p in range(near):
                copies.append(
                    pltpu.make_async_copy(
                        kept_ref.at[i, p, :, lanes], kept_out[i * near + p].at[:, lanes], out_sem.at[step, i * near + p]
                    )
                )
        return copies

    small = [
        pltpu.make_async_copy(z_tables_ref, z_ref, table_sem.at[0]),
        pltpu.make_async_copy(x_tables, x_ref, table_sem.at[1]),
        pltpu.make_async_copy(y_tables, y_ref, table_sem.at[2]),
    ]
    k_copy = pltpu.make_async_copy(kern, k_ref, table_sem.at[3])
    kept_copies = []
    if kept_held:
        for i in range(a_count):
            for p in range(near):
                kept_copies.append(
                    pltpu.make_async_copy(kept_in[i][p], kept_ref.at[i, p], kept_sem.at[i * near + p])
                )

    small[0].start()
    small[1].start()

    for part in range(CHUNKS):
        for p in range(len(pieces)):
            piece_in(part, p).start()
    small[2].start()
    k_copy.start()
    for copy in kept_copies:
        copy.start()

    spans_cut, spans_lay, at = [], [], 0
    for t0, t1 in lines:
        spans_cut.append(slice(at, at + 2 * (t1 - t0) * LANES))
        at += 2 * (t1 - t0) * LANES
    for s0, s1 in tiles:
        spans_lay.append(slice(at, at + 2 * (s1 - s0) * LANES))
        at += 2 * (s1 - s0) * LANES

    def stack(first, number, lanes):
        return jnp.concatenate([held[first + p, :, lanes].astype(F32) for p in range(number)], axis=0)

    small[0].wait()
    small[1].wait()

    def forward(step, carry):
        for part in range(CHUNKS):

            @pl.when(step == part * steps // CHUNKS)
            def _():
                for p in range(len(pieces)):
                    piece_in(part, p).wait()

        rho = [[], []]
        for g in range(GROUPS):
            lanes = pl.ds(pl.multiple_of((step * GROUPS + g) * width, LANES), width)
            a = [stack(i * n, n, lanes) for i in range(a_count)]
            b = [stack((a_count + j) * n, n, lanes) for j in range(b_count)]
            for k, (i, j) in enumerate(pairs):
                rho[k].append((a[i] * b[j]).astype(BF))
        rho = [jnp.concatenate(r, axis=0) for r in rho]
        along = []
        for s, (t0, t1) in enumerate(lines):
            lhs = jnp.concatenate([r[:, t0 * LANES:t1 * LANES] for r in rho], axis=1)
            along.append(dot(lhs, z_ref[spans_cut[s], :]).astype(BF))
        for g in range(GROUPS):
            parts = []
            for s in range(per):
                w = along[s][g * count:(g + 1) * count]
                parts.append(jnp.concatenate([w[:, :LANES], w[:, LANES:]], axis=0))
            out = dot(x_ref[:2 * count], jnp.concatenate(parts, axis=1))
            y = (step * GROUPS + g) * per
            for s in range(per):
                s_ref[pl.ds(y + s, 2 * count, pitch), :] = out[:, s * LANES:(s + 1) * LANES]
        return carry

    lax.fori_loop(0, steps, forward, 0)
    small[2].wait()
    k_copy.wait()

    def plane_set(ref, first):
        return jnp.concatenate(
            [
                jnp.concatenate(
                    [ref[pl.ds((c * count + first + e) * pitch, count), :].astype(BF) for c in range(2)], axis=0
                )
                for e in range(per)
            ],
            axis=1,
        )

    def middle(step, carry):
        firsts = [(step * UNROLL + u) * per for u in range(UNROLL)]
        summed = [dot(y_ref[:2 * count], plane_set(s_ref, gx)) for gx in firsts]
        spectra = []
        for gx, value in zip(firsts, summed):
            scale = jnp.concatenate([k_ref[gx + e] for e in range(per)], axis=1)
            spectra.append(
                jnp.concatenate([(value[:count] * scale).astype(BF), (value[count:] * scale).astype(BF)], axis=0)
            )
        backs = [dot(y_ref[2 * count:], spectrum) for spectrum in spectra]
        for gx, value in zip(firsts, backs):
            for e in range(per):
                r_ref[pl.ds(gx + e, 2 * count, pitch), :] = value[:, e * LANES:(e + 1) * LANES]
        return carry

    lax.fori_loop(0, count // (per * UNROLL), middle, 0)
    for copy in kept_copies:
        copy.wait()

    def backward(step, carry):
        columns = []
        for g in range(GROUPS):
            out = dot(x_ref[2 * count:], plane_set(r_ref, (step * GROUPS + g) * per)).astype(BF)
            row = []
            for s in range(per):
                w = out[:, s * LANES:(s + 1) * LANES]
                row.append(jnp.concatenate([w[:planes], w[planes:]], axis=1))
            columns.append(row)
        for t, (s0, s1) in enumerate(tiles):
            lhs = jnp.concatenate([jnp.concatenate(row[s0:s1], axis=1) for row in columns], axis=0)
            potential = dot(lhs, z_ref[spans_lay[t], :])
            for g in range(GROUPS):
                lanes = pl.ds(pl.multiple_of((step * GROUPS + g) * width + t * LANES, LANES), LANES)
                minus = -potential[g * planes:(g + 1) * planes]
                a = [stack(i * n, near, lanes) for i in range(a_count)]
                b = [stack((a_count + j) * n, near, lanes) for j in range(b_count)]
                sent, kept = [None] * b_count, [None] * a_count
                for k, (i, j) in enumerate(pairs):
                    v = minus[:, k * LANES:(k + 1) * LANES]
                    sent[j] = v * a[i] if sent[j] is None else sent[j] + v * a[i]
                    kept[i] = v * b[j] if kept[i] is None else kept[i] + v * b[j]
                for p in range(near):
                    part = slice(p * rows, (p + 1) * rows)
                    for j in range(b_count):
                        if p:
                            sent_rest[j, p - 1, :, lanes] = sent[j][part].astype(BF)
                        else:
                            sent_near[j, :, lanes] = sent[j][part]
                    for i in range(a_count):
                        value = kept[i][part]
                        if kept_held:
                            value = value + kept_ref[i, p, :, lanes]
                        kept_ref[i, p, :, lanes] = value
        for part in range(CHUNKS):

            @pl.when(step == (part + 1) * steps // CHUNKS - 1)
            def _():
                for copy in outgoing(part):
                    copy.start()

        return carry

    lax.fori_loop(0, steps, backward, 0)

    for part in range(CHUNKS):
        for copy in outgoing(part):
            copy.wait()


def unit(a, b, core, kern, x_tables, near, kept_in):
    count = kern.shape[0]
    n = len(a[0])
    rows, width = a[0][0][0].shape[1:]
    a_count, b_count = len(a), len(b)
    y_tables = np.concatenate([half(t) for t in complex_tables(count)], axis=0)
    cut, lay = z_tables(count)
    z_all = np.concatenate([*cut, *lay], axis=0)
    chosen = [r for pieces in (*a, *b) for r in pieces]
    ins = [r[0] for r in chosen] + [kern, x_tables, y_tables, z_all]
    if kept_in is not None:
        ins += [k for pieces in kept_in for k in pieces]
    anywhere = pl.BlockSpec(memory_space=pltpu.HBM)
    pieces = (a_count + b_count) * n
    outs = pl.pallas_call(
        functools.partial(
            unit_body, count, n, near, a_count, b_count, [r[1:] for r in chosen], kept_in is not None
        ),
        out_shape=[
            jax.ShapeDtypeStruct((rows, width), BF if p else F32) for _ in range(b_count) for p in range(near)
        ]
        + [jax.ShapeDtypeStruct((rows, width), F32)] * (a_count * near),
        in_specs=[pl.BlockSpec(memory_space=pltpu.SMEM)] + [anywhere] * len(ins),
        out_specs=[anywhere] * ((a_count + b_count) * near),
        scratch_shapes=[
            pltpu.VMEM((pieces, rows, width), BF),
            pltpu.VMEM(kern.shape, F32),
            pltpu.VMEM(x_tables.shape, BF),
            pltpu.VMEM(y_tables.shape, BF),
            pltpu.VMEM(z_all.shape, BF),
            pltpu.VMEM((b_count, rows, width), F32),
            pltpu.VMEM((b_count, near - 1, rows, width), BF),
            pltpu.VMEM((a_count, near, rows, width), F32),
            pltpu.VMEM((2 * count * (count + PITCH), LANES), F32),
            pltpu.VMEM((2 * count * (count + PITCH), LANES), F32),
            pltpu.SemaphoreType.DMA((CHUNKS, pieces)),
            pltpu.SemaphoreType.DMA((4,)),
            pltpu.SemaphoreType.DMA((a_count * near,)),
            pltpu.SemaphoreType.DMA((CHUNKS, b_count * near)),
            pltpu.SemaphoreType.DMA((CHUNKS, a_count * near)),
        ],
        compiler_params=pltpu.CompilerParams(vmem_limit_bytes=VMEM_BYTES),
        cost_estimate=pl.CostEstimate(flops=FLOPS, bytes_accessed=10**3, transcendentals=0),
        name="pair_potentials",
    )(core, *ins)
    sent = [outs[j * near:(j + 1) * near] for j in range(b_count)]
    kept = [outs[(b_count + i) * near:(b_count + i + 1) * near] for i in range(a_count)]
    return sent, kept


def split_of(n):
    gb = 1
    while gb * gb < n and gb < 4:
        gb *= 2
    return n // gb, gb


def after(value, *events):
    return lax.optimization_barrier((value, *events))[0]


def local(orbitals, kernel, *, ga, gb):
    band_count, rows, width = orbitals.shape
    n = ga * gb
    count = rows * n
    na = band_count // gb
    blocks = lax.axis_size("band")
    me = lax.axis_index("grid")
    bi = me % gb

    def hop(x, distance):
        return lax.ppermute(x, "band", [(i, (i + distance) % blocks) for i in range(blocks)])

    def to_a(x, s):
        return lax.ppermute(x, "grid", [(((i // gb + s) % ga) * gb + i % gb, i) for i in range(n)])

    def to_b(x, t):
        return lax.ppermute(x, "grid", [((i // gb) * gb + (i % gb + t) % gb, i) for i in range(n)])

    order = [(s, t) for s in range(ga) for t in range(gb)]
    fwd, bwd, mirror = device_tables(count, ga, gb)
    x_tables, mirror = (
        lax.dynamic_index_in_dim(jnp.asarray(t), me, 0, False) for t in (np.concatenate([fwd, bwd], axis=1), mirror)
    )

    core = bi.astype(jnp.int32).reshape(1)

    def others(x):
        return [to_b(x, t) for t in range(1, gb)]

    k_own = kernel.astype(BF)
    shares = [orbitals[index * gb:(index + 1) * gb] for index in range(na)]
    singles = [orbitals[j:j + 1] for j in range(gb, band_count)]
    own_near = [orbitals, *others(orbitals)]
    k_near = [k_own, *others(k_own)]
    k_far = [to_a(k_own, s) for s in range(1, ga)]
    own_far = [[to_a(shares[0], s) for s in range(1, ga)]]
    block = hop(shares[0], DIST)
    landed = [hop(x, DIST) for x in singles[:1]]
    k_far, own_far, block, landed, shares, singles, own_near, k_near, x_tables, mirror = lax.optimization_barrier(
        (k_far, own_far, block, landed, shares, singles, own_near, k_near, x_tables, mirror)
    )

    own_far += [[to_a(shares[index], s) for s in range(1, ga)] for index in range(1, na)]
    forwarded = [hop(r[:1], DIST) for r in own_far[0]]
    k_rows = list(k_near)
    for r in k_far:
        k_rows += [r, *others(r)]
    kern = whole_kernel(k_rows, mirror, count)
    far_pieces = [[[r, *others(r)] for r in own_far[0]]]
    near_blocks = [[x, *others(x)] for x in [block, *landed[:1]]]
    own_far, forwarded, singles, kern, far_pieces, near_blocks = lax.optimization_barrier(
        (own_far, forwarded, singles, kern, far_pieces, near_blocks)
    )

    far_pieces += [[[r, *others(r)] for r in own_far[index]] for index in range(1, na)]
    landed = [hop(x, DIST) for x in singles[1:]]
    near_blocks += [[x, *others(x)] for x in landed]
    own = []
    for index in range(na):
        pieces = [(r, 1, index * gb) for r in own_near]
        pieces += [(r, 1, 0) for group in far_pieces[index] for r in group]
        own.append(pieces)
    near = [[(r, 0, j) for r in near_blocks[0]] for j in range(gb)]
    near += [[(r, 0, 0) for r in blocks_near] for blocks_near in near_blocks[1:]]

    def partner(j, *events):
        pieces = list(near[j])
        for s in range(1, ga):
            if j == 0:
                r = forwarded[s - 1]
            else:
                r, _, offset = near[j][0]
                r = to_a(r[offset:offset + 1], s)
                if events:
                    r = after(r, *events)
            pieces += [(x, 0, 0) for x in [r, *others(r)]]
        return pieces

    returned = [None] * band_count
    events = []

    def send_back(sent, j):
        total = sent[0]
        for t in range(1, gb):
            total = total + to_b(sent[t], gb - t).astype(F32)
        total = total.astype(BF)
        events.append(total)
        returned[j] = hop(total, -DIST)

    kept = None
    sent_by = []
    per_unit = 2 // na
    for u in range(0, band_count, per_unit):
        b = [partner(j, *(sent_by[-2:-1] or sent_by)) for j in range(u, u + per_unit)]
        tables = after(x_tables, events[-2]) if len(events) > 1 else x_tables
        sent, kept = unit(own, b, core, kern, tables, gb, kept)
        sent_by.append(sent[0][0])
        for e in range(per_unit):
            send_back(sent[e], u + e)

    parts = [[x[0] for x in kept]]
    for t in range(1, gb):
        received = to_b(jnp.stack([x[t] for x in kept]).astype(BF), gb - t)
        parts.append([received[index].astype(F32) for index in range(na)])
    rows_out = []
    for j in range(band_count):
        index, owner = divmod(j, gb)
        which = (bi - owner + gb) % gb
        value = parts[0][index]
        for t in range(1, gb):
            value = jnp.where(which == t, parts[t][index], value)
        rows_out.append(value)
    early = band_count - per_unit
    base = lax.optimization_barrier(
        jnp.stack([v + returned[j].astype(F32) if j < early else v for j, v in enumerate(rows_out)])
    )
    last = base[early:] + jnp.stack(returned[early:]).astype(F32)
    return lax.dynamic_update_slice(base, last, (early, 0, 0))


def solution(mesh):
    ga, gb = split_of(mesh.shape["grid"])
    placed = (P("band", "grid", None), P("grid", None))
    return jax.shard_map(
        functools.partial(local, ga=ga, gb=gb),
        mesh=mesh,
        in_specs=placed,
        out_specs=P("band", "grid", None),
        check_vma=False,
    )
```

```python
import functools

import jax
import jax.numpy as jnp
import ml_dtypes
import numpy as np
from jax import lax
from jax.experimental import pallas as pl
from jax.experimental.pallas import tpu as pltpu
from jax.sharding import PartitionSpec as P

DIST = 1
LANES = 128
TILES = 3
GROUPS = 12
UNROLL = 12
CHUNKS = 2
PITCH = 4
BF = jnp.bfloat16
F32 = jnp.float32
FLOPS = 10**11
VMEM_BYTES = 62 * 1024 * 1024


def dot(a, b):
    return jnp.dot(a, b, preferred_element_type=F32)


def half(a):
    return np.asarray(a, np.float32).astype(ml_dtypes.bfloat16)


def complex_tables(count):
    j = np.arange(count)
    angles = (j[:, None] * j[None, :] % count).astype(np.float32) * np.float32(2.0 * np.pi / count)
    cosine = half(np.cos(angles)).astype(np.float32)
    sine = half(np.sin(angles)).astype(np.float32)
    forward = np.block([[cosine, sine], [-sine, cosine]])
    backward = np.block([[cosine, -sine], [sine, cosine]])
    return forward, backward


def line_spans(count):
    per = TILES * LANES // count
    lines = [(s * count // LANES, -(-(s + 1) * count // LANES)) for s in range(per)]
    tiles = [(t * LANES // count, -(-(t + 1) * LANES // count)) for t in range(TILES)]
    return lines, tiles


def z_tables(count):
    forward, backward = complex_tables(count)
    lines, tiles = line_spans(count)
    cut, lay = [], []
    for s, (t0, t1) in enumerate(lines):
        w = np.zeros((2, (t1 - t0) * LANES, 2, LANES), np.float32)
        first = s * count - t0 * LANES
        for c in range(2):
            for d in range(2):
                w[c, first:first + count, d, :count] = forward[d * count:(d + 1) * count, c * count:(c + 1) * count].T
        cut.append(half(w.reshape(-1, 2 * LANES)))
    for t, (s0, s1) in enumerate(tiles):
        w = np.zeros((s1 - s0, 2, LANES, 2, LANES), np.float32)
        for s in range(s0, s1):
            for z in range(count):
                lane = s * count + z - t * LANES
                if 0 <= lane < LANES:
                    for c in range(2):
                        for d in range(2):
                            w[s - s0, c, :count, d, lane] = backward[d * count + z, c * count:(c + 1) * count]
        lay.append(half(w.reshape(-1, 2 * LANES)))
    return cut, lay


def piece_planes(count, ga, gb, device):
    rows = count // (ga * gb)
    ai, bi = divmod(device, gb)
    owners = [((ai + s) % ga) * gb + (bi + t) % gb for s in range(ga) for t in range(gb)]
    return np.concatenate([np.arange(o * rows, (o + 1) * rows) for o in owners])


def device_tables(count, ga, gb):
    forward, backward = complex_tables(count)
    near = count // ga
    fwd, bwd, mirror = [], [], []
    for device in range(ga * gb):
        planes = piece_planes(count, ga, gb, device)
        fwd.append(np.concatenate([forward[:, planes], forward[:, count + planes]], axis=1))
        bwd.append(np.concatenate([backward[planes[:near]], backward[count + planes[:near]]], axis=0))
        place = np.eye(count, dtype=np.float32)[:, planes]
        flip = place[(-np.arange(count)) % count]
        mirror.append(np.concatenate([place, flip], axis=1))
    return half(np.stack(fwd)), half(np.stack(bwd)), half(np.stack(mirror))


def line_selectors(count):
    lines, _ = line_spans(count)
    picks = []
    for s, (t0, t1) in enumerate(lines):
        w = np.zeros(((t1 - t0) * LANES, 2, LANES), np.float32)
        for z in range(count):
            w[s * count + z - t0 * LANES, 0, z] = 1
            w[s * count + z - t0 * LANES, 1, (-z) % count] = 1
        picks.append(half(w.reshape(-1, 2 * LANES)))
    return picks


def kernel_body(count, n, place_ref, *refs):
    pieces, mirror = refs[:n], refs[n]
    lines, _ = line_spans(count)
    picks = refs[n + 1:n + 1 + len(lines)]
    out_ref, cut_ref = refs[n + 1 + len(lines):]
    per = len(lines)
    width = TILES * LANES
    unrolled = 6

    def cut(step, carry):
        for u in range(unrolled):
            group = step * unrolled + u
            lanes = pl.ds(pl.multiple_of(group * width, LANES), width)
            k = jnp.concatenate([r[:, lanes].astype(F32) for r in pieces], axis=0).astype(BF)
            for s, (t0, t1) in enumerate(lines):
                cut_ref[group * per + s] = dot(k[:, t0 * LANES:t1 * LANES], picks[s][...]).astype(BF)
        return carry

    lax.fori_loop(0, count // (per * unrolled), cut, 0)

    def join(step, carry):
        for u in range(0, 16, 2):
            both = []
            for e in range(2):
                gx = step * 16 + u + e
                back = lax.rem(count - gx, count)
                both.append(jnp.concatenate([cut_ref[gx][:, :LANES], cut_ref[back][:, LANES:]], axis=0))
            value = dot(mirror[place_ref[0]], jnp.concatenate(both, axis=1)) * (0.5 / count**3)
            for e in range(2):
                out_ref[step * 16 + u + e] = value[:, e * LANES:(e + 1) * LANES]
        return carry

    lax.fori_loop(0, count // 16, join, 0)


def whole_kernel(pieces, place, mirror, count):
    picks = line_selectors(count)
    vmem = pl.BlockSpec(memory_space=pltpu.VMEM)
    ins = [*pieces, mirror, *picks]
    return pl.pallas_call(
        functools.partial(kernel_body, count, len(pieces)),
        out_shape=jax.ShapeDtypeStruct((count, count, LANES), F32),
        in_specs=[pl.BlockSpec(memory_space=pltpu.SMEM)] + [vmem] * len(ins),
        out_specs=vmem,
        scratch_shapes=[pltpu.VMEM((count, count, 2 * LANES), BF)],
        compiler_params=pltpu.CompilerParams(vmem_limit_bytes=VMEM_BYTES),
        cost_estimate=pl.CostEstimate(flops=FLOPS, bytes_accessed=10**3, transcendentals=0),
        name="symmetric_kernel",
    )(place, *ins)


def unit_body(count, n, near, a_count, b_count, places, kept_held, place_ref, *refs):
    refs = list(refs)

    def take(k):
        return [refs.pop(0) for _ in range(k)]

    lines, tiles = line_spans(count)
    per = len(lines)
    width = TILES * LANES
    pieces = take((a_count + b_count) * n)
    kern, x_tables, y_tables, z_tables_ref = take(4)
    kept_in = [take(near) for _ in range(a_count)] if kept_held else None
    sent_out, kept_out = take(b_count * near), take(a_count * near)
    held, k_ref, x_ref, y_ref, z_ref, sent_near, sent_rest, kept_ref, s_ref, r_ref = take(10)
    in_sem, table_sem, kept_sem, sent_sem, out_sem = take(5)
    rows = pieces[0].shape[1]
    core = lax.rem(place_ref[0], near)
    where = [core * step + offset if step else offset for step, offset in places]
    pitch = count + PITCH
    planes = near * rows
    steps = count // (per * GROUPS)
    chunk = count * count // CHUNKS
    pairs = [(i, j) for i in range(a_count) for j in range(b_count)]

    def lanes_of(part):
        return slice(part * chunk, (part + 1) * chunk)

    def piece_in(step, p):
        return pltpu.make_async_copy(
            pieces[p].at[where[p], :, lanes_of(step)], held.at[p, :, lanes_of(step)], in_sem.at[step, p]
        )

    def outgoing(step):
        lanes = lanes_of(step)
        copies = []
        for j in range(b_count):
            for p in range(near):
                source = sent_rest.at[j, p - 1, :, lanes] if p else sent_near.at[j, :, lanes]
                copies.append(
                    pltpu.make_async_copy(source, sent_out[j * near + p].at[:, lanes], sent_sem.at[step, j * near + p])
                )
        for i in range(a_count):
            for p in range(near):
                copies.append(
                    pltpu.make_async_copy(
                        kept_ref.at[i, p, :, lanes], kept_out[i * near + p].at[:, lanes], out_sem.at[step, i * near + p]
                    )
                )
        return copies

    small = [
        pltpu.make_async_copy(z_tables_ref, z_ref, table_sem.at[0]),
        pltpu.make_async_copy(x_tables.at[place_ref[0]], x_ref, table_sem.at[1]),
        pltpu.make_async_copy(y_tables, y_ref, table_sem.at[2]),
    ]
    k_copy = pltpu.make_async_copy(kern, k_ref, table_sem.at[3])
    kept_copies = []
    if kept_held:
        for i in range(a_count):
            for p in range(near):
                kept_copies.append(
                    pltpu.make_async_copy(kept_in[i][p], kept_ref.at[i, p], kept_sem.at[i * near + p])
                )

    small[0].start()
    small[1].start()

    for part in range(CHUNKS):
        for p in range(len(pieces)):
            piece_in(part, p).start()
    small[2].start()
    k_copy.start()
    for copy in kept_copies:
        copy.start()

    spans_cut, spans_lay, at = [], [], 0
    for t0, t1 in lines:
        spans_cut.append(slice(at, at + 2 * (t1 - t0) * LANES))
        at += 2 * (t1 - t0) * LANES
    for s0, s1 in tiles:
        spans_lay.append(slice(at, at + 2 * (s1 - s0) * LANES))
        at += 2 * (s1 - s0) * LANES

    def stack(first, number, lanes):
        return jnp.concatenate([held[first + p, :, lanes].astype(F32) for p in range(number)], axis=0)

    small[0].wait()
    small[1].wait()

    def forward(step, carry):
        for part in range(CHUNKS):

            @pl.when(step == part * steps // CHUNKS)
            def _():
                for p in range(len(pieces)):
                    piece_in(part, p).wait()

        rho = [[], []]
        for g in range(GROUPS):
            lanes = pl.ds(pl.multiple_of((step * GROUPS + g) * width, LANES), width)
            a = [stack(i * n, n, lanes) for i in range(a_count)]
            b = [stack((a_count + j) * n, n, lanes) for j in range(b_count)]
            for k, (i, j) in enumerate(pairs):
                rho[k].append((a[i] * b[j]).astype(BF))
        rho = [jnp.concatenate(r, axis=0) for r in rho]
        along = []
        for s, (t0, t1) in enumerate(lines):
            lhs = jnp.concatenate([r[:, t0 * LANES:t1 * LANES] for r in rho], axis=1)
            along.append(dot(lhs, z_ref[spans_cut[s], :]).astype(BF))
        for g in range(GROUPS):
            parts = []
            for s in range(per):
                w = along[s][g * count:(g + 1) * count]
                parts.append(jnp.concatenate([w[:, :LANES], w[:, LANES:]], axis=0))
            out = dot(x_ref[:2 * count], jnp.concatenate(parts, axis=1))
            y = (step * GROUPS + g) * per
            for s in range(per):
                s_ref[pl.ds(y + s, 2 * count, pitch), :] = out[:, s * LANES:(s + 1) * LANES]
        return carry

    lax.fori_loop(0, steps, forward, 0)
    small[2].wait()
    k_copy.wait()

    def plane_set(ref, first):
        return jnp.concatenate(
            [
                jnp.concatenate(
                    [ref[pl.ds((c * count + first + e) * pitch, count), :].astype(BF) for c in range(2)], axis=0
                )
                for e in range(per)
            ],
            axis=1,
        )

    def middle(step, carry):
        firsts = [(step * UNROLL + u) * per for u in range(UNROLL)]
        summed = [dot(y_ref[:2 * count], plane_set(s_ref, gx)) for gx in firsts]
        spectra = []
        for gx, value in zip(firsts, summed):
            scale = jnp.concatenate([k_ref[gx + e] for e in range(per)], axis=1)
            spectra.append(
                jnp.concatenate([(value[:count] * scale).astype(BF), (value[count:] * scale).astype(BF)], axis=0)
            )
        backs = [dot(y_ref[2 * count:], spectrum) for spectrum in spectra]
        for gx, value in zip(firsts, backs):
            for e in range(per):
                r_ref[pl.ds(gx + e, 2 * count, pitch), :] = value[:, e * LANES:(e + 1) * LANES]
        return carry

    lax.fori_loop(0, count // (per * UNROLL), middle, 0)
    for copy in kept_copies:
        copy.wait()

    def backward(step, carry):
        columns = []
        for g in range(GROUPS):
            out = dot(x_ref[2 * count:], plane_set(r_ref, (step * GROUPS + g) * per)).astype(BF)
            row = []
            for s in range(per):
                w = out[:, s * LANES:(s + 1) * LANES]
                row.append(jnp.concatenate([w[:planes], w[planes:]], axis=1))
            columns.append(row)
        for t, (s0, s1) in enumerate(tiles):
            lhs = jnp.concatenate([jnp.concatenate(row[s0:s1], axis=1) for row in columns], axis=0)
            potential = dot(lhs, z_ref[spans_lay[t], :])
            for g in range(GROUPS):
                lanes = pl.ds(pl.multiple_of((step * GROUPS + g) * width + t * LANES, LANES), LANES)
                minus = -potential[g * planes:(g + 1) * planes]
                a = [stack(i * n, near, lanes) for i in range(a_count)]
                b = [stack((a_count + j) * n, near, lanes) for j in range(b_count)]
                sent, kept = [None] * b_count, [None] * a_count
                for k, (i, j) in enumerate(pairs):
                    v = minus[:, k * LANES:(k + 1) * LANES]
                    sent[j] = v * a[i] if sent[j] is None else sent[j] + v * a[i]
                    kept[i] = v * b[j] if kept[i] is None else kept[i] + v * b[j]
                for p in range(near):
                    part = slice(p * rows, (p + 1) * rows)
                    for j in range(b_count):
                        if p:
                            sent_rest[j, p - 1, :, lanes] = sent[j][part].astype(sent_rest.dtype)
                        else:
                            sent_near[j, :, lanes] = sent[j][part]
                    for i in range(a_count):
                        value = kept[i][part]
                        if kept_held:
                            value = value + kept_ref[i, p, :, lanes]
                        kept_ref[i, p, :, lanes] = value
        for part in range(CHUNKS):

            @pl.when(step == (part + 1) * steps // CHUNKS - 1)
            def _():
                for copy in outgoing(part):
                    copy.start()

        return carry

    lax.fori_loop(0, steps, backward, 0)

    for part in range(CHUNKS):
        for copy in outgoing(part):
            copy.wait()


def unit(a, b, place, kern, x_tables, near, kept_in):
    count = kern.shape[0]
    n = len(a[0])
    rows, width = a[0][0][0].shape[1:]
    a_count, b_count = len(a), len(b)
    y_tables = np.concatenate([half(t) for t in complex_tables(count)], axis=0)
    cut, lay = z_tables(count)
    z_all = np.concatenate([*cut, *lay], axis=0)
    chosen = [r for pieces in (*a, *b) for r in pieces]
    ins = [r[0] for r in chosen] + [kern, x_tables, y_tables, z_all]
    if kept_in is not None:
        ins += [k for pieces in kept_in for k in pieces]
    anywhere = pl.BlockSpec(memory_space=pltpu.HBM)
    pieces = (a_count + b_count) * n
    outs = pl.pallas_call(
        functools.partial(
            unit_body, count, n, near, a_count, b_count, [r[1:] for r in chosen], kept_in is not None
        ),
        out_shape=[
            jax.ShapeDtypeStruct((rows, width), BF if p else F32) for _ in range(b_count) for p in range(near)
        ]
        + [jax.ShapeDtypeStruct((rows, width), F32)] * (a_count * near),
        in_specs=[pl.BlockSpec(memory_space=pltpu.SMEM)] + [anywhere] * len(ins),
        out_specs=[anywhere] * ((a_count + b_count) * near),
        scratch_shapes=[
            pltpu.VMEM((pieces, rows, width), BF),
            pltpu.VMEM(kern.shape, F32),
            pltpu.VMEM(x_tables.shape[1:], BF),
            pltpu.VMEM(y_tables.shape, BF),
            pltpu.VMEM(z_all.shape, BF),
            pltpu.VMEM((b_count, rows, width), F32),
            pltpu.VMEM((b_count, near - 1, rows, width), BF),
            pltpu.VMEM((a_count, near, rows, width), F32),
            pltpu.VMEM((2 * count * (count + PITCH), LANES), F32),
            pltpu.VMEM((2 * count * (count + PITCH), LANES), F32),
            pltpu.SemaphoreType.DMA((CHUNKS, pieces)),
            pltpu.SemaphoreType.DMA((4,)),
            pltpu.SemaphoreType.DMA((a_count * near,)),
            pltpu.SemaphoreType.DMA((CHUNKS, b_count * near)),
            pltpu.SemaphoreType.DMA((CHUNKS, a_count * near)),
        ],
        compiler_params=pltpu.CompilerParams(vmem_limit_bytes=VMEM_BYTES),
        cost_estimate=pl.CostEstimate(flops=FLOPS, bytes_accessed=10**3, transcendentals=0),
        name="pair_potentials",
    )(place, *ins)
    sent = [outs[j * near:(j + 1) * near] for j in range(b_count)]
    kept = [outs[(b_count + i) * near:(b_count + i + 1) * near] for i in range(a_count)]
    return sent, kept


def split_of(n):
    gb = 1
    while gb * gb < n and gb < 4:
        gb *= 2
    return n // gb, gb


def after(value, *events):
    return lax.optimization_barrier((value, *events))[0]


def local(orbitals, kernel, *, ga, gb):
    band_count, rows, width = orbitals.shape
    n = ga * gb
    count = rows * n
    na = band_count // gb
    blocks = lax.axis_size("band")
    me = lax.axis_index("grid")
    bi = me % gb

    def hop(x, distance):
        return lax.ppermute(x, "band", [(i, (i + distance) % blocks) for i in range(blocks)])

    def to_a(x, s):
        return lax.ppermute(x, "grid", [(((i // gb + s) % ga) * gb + i % gb, i) for i in range(n)])

    def to_b(x, t):
        return lax.ppermute(x, "grid", [((i // gb) * gb + (i % gb + t) % gb, i) for i in range(n)])

    order = [(s, t) for s in range(ga) for t in range(gb)]
    fwd, bwd, mirror = device_tables(count, ga, gb)
    x_tables = jnp.asarray(np.concatenate([fwd, bwd], axis=1))

    place = me.astype(jnp.int32).reshape(1)

    def others(x):
        return [to_b(x, t) for t in range(1, gb)]

    own_near = [orbitals, *others(orbitals)]
    late = after(orbitals, own_near[1])
    rest = [late[gb + 1:]] if na > 1 else []
    first_near = late[:gb + 1] if na > 1 else orbitals
    k_own = kernel.astype(BF)
    k_near = [k_own, *others(k_own)]
    k_far = [to_a(k_own, s) for s in range(1, ga)]
    block = hop(first_near, DIST)
    first_own = [to_a(orbitals[:gb], s) for s in range(1, ga)]
    first_own, rest, own_near, k_far = lax.optimization_barrier((first_own, rest, own_near, k_far))
    shares = [after(orbitals, *first_own)[index * gb:(index + 1) * gb] if index else None for index in range(na)]
    if na > 1:
        k_far = [after(r, *shares[1:]) for r in k_far]

    k_rows = list(k_near)
    for r in k_far:
        k_rows += [r, *others(r)]
    kern = whole_kernel(k_rows, place, after(jnp.asarray(mirror), block), count)
    near_blocks = [[x, *others(x)] for x in [block]]
    far_pieces = [[[r, *others(r)] for r in first_own]]
    forwarded = [hop(r, DIST) for r in first_own]
    later_far = [[to_a(shares[index], s) for s in range(1, ga)] for index in range(1, na)]
    later_far, forwarded, kern, rest = lax.optimization_barrier((later_far, forwarded, kern, rest))
    far_pieces += [[[r, *others(r)] for r in far] for far in later_far]
    first_far = [[r, *others(r)] for r in forwarded]
    landed = [hop(x, DIST) for x in rest]

    own = []
    for index in range(na):
        pieces = [(r, 1, index * gb) for r in own_near]
        pieces += [(r, 1, 0) for group in far_pieces[index] for r in group]
        own.append(pieces)
    near = [[(r, 0, j) for r in near_blocks[0]] for j in range(first_near.shape[0])]

    def partner(j, *events):
        if j < gb:
            return near[j] + [(x, 0, j) for group in first_far for x in group]
        pieces = list(near[j]) if j < len(near) else [(r, 0, 0) for r in [landed[0], *others(landed[0])]]
        for s in range(1, ga):
            x = to_a(singles[j], s)
            x = after(x, sent_by[j - gb])
            pieces += [(y, 0, 0) for y in [x, *others(x)]]
        return pieces

    returned = [None] * band_count
    events = []

    def send_back(sent, j):
        if j == band_count - 1 and per_unit == 1:
            sent = [sent[0], *(after(x, returned[j - 2]) for x in sent[1:])]
        total = sent[0]
        for t in range(1, gb):
            total = total + to_b(sent[t], gb - t).astype(F32)
        total = total.astype(BF)
        events.append(total)
        returned[j] = hop(total, -DIST)

    per_unit = 2 // na
    kept = None
    sent_by = []
    one = lax.optimization_barrier(jnp.ones((), BF))
    singles = {}
    for u in range(0, band_count, per_unit):
        b = [partner(j) for j in range(u, u + per_unit)]
        waits = []
        if u > 1 and per_unit == 1:
            waits = [*events[max(u - 2, 0):u if u == band_count - 1 else u - 1], *returned[:u - 2]]
        if na > 1 and u < 2:
            if u:
                landed[0] = after(landed[0], sent_by[-1])
            singles[gb + u] = landed[0] * one if u else after(block, later_far)[gb:gb + 1]
            waits = [*waits, singles[gb + u]]
        tables = after(x_tables, *waits) if waits else x_tables
        sent, kept = unit(own, b, place, kern, tables, gb, kept)
        sent_by.append(sent[0][0])
        for e in range(per_unit):
            send_back(sent[e], u + e)

    parts = [[x[0] for x in kept]]
    for t in range(1, gb):
        received = to_b(jnp.stack([x[t] for x in kept]).astype(BF), gb - t)
        parts.append([received[index].astype(F32) for index in range(na)])
    rows_out = []
    for j in range(band_count):
        index, owner = divmod(j, gb)
        which = (bi - owner + gb) % gb
        value = parts[0][index]
        for t in range(1, gb):
            value = jnp.where(which == t, parts[t][index], value)
        rows_out.append(value)
    early = band_count - per_unit
    base = lax.optimization_barrier(
        jnp.stack([v + returned[j].astype(F32) if j < early else v for j, v in enumerate(rows_out)])
    )
    last = base[early:] + jnp.stack(returned[early:]).astype(F32)
    return lax.dynamic_update_slice(base, last, (early, 0, 0))


def solution(mesh):
    ga, gb = split_of(mesh.shape["grid"])
    placed = (P("band", "grid", None), P("grid", None))
    return jax.shard_map(
        functools.partial(local, ga=ga, gb=gb),
        mesh=mesh,
        in_specs=placed,
        out_specs=P("band", "grid", None),
        check_vma=False,
    )
```

```python
import functools

import jax
import jax.numpy as jnp
import ml_dtypes
import numpy as np
from jax import lax
from jax.experimental import pallas as pl
from jax.experimental.pallas import tpu as pltpu
from jax.sharding import PartitionSpec as P

DIST = 1
LANES = 128
TILES = 3
GROUPS = 12
UNROLL = 24
CHUNKS = 2
PITCH = 4
BF = jnp.bfloat16
F32 = jnp.float32
FLOPS = 10**11
VMEM_BYTES = 62 * 1024 * 1024


def dot(a, b):
    return jnp.dot(a, b, preferred_element_type=F32)


def half(a):
    return np.asarray(a, np.float32).astype(ml_dtypes.bfloat16)


def complex_tables(count):
    j = np.arange(count)
    angles = (j[:, None] * j[None, :] % count).astype(np.float32) * np.float32(2.0 * np.pi / count)
    cosine = half(np.cos(angles)).astype(np.float32)
    sine = half(np.sin(angles)).astype(np.float32)
    forward = np.block([[cosine, sine], [-sine, cosine]])
    backward = np.block([[cosine, -sine], [sine, cosine]])
    return forward, backward


def line_spans(count):
    per = TILES * LANES // count
    lines = [(s * count // LANES, -(-(s + 1) * count // LANES)) for s in range(per)]
    tiles = [(t * LANES // count, -(-(t + 1) * LANES // count)) for t in range(TILES)]
    return lines, tiles


def z_tables(count):
    forward, backward = complex_tables(count)
    lines, tiles = line_spans(count)
    cut, lay = [], []
    for s, (t0, t1) in enumerate(lines):
        w = np.zeros((2, (t1 - t0) * LANES, 2, LANES), np.float32)
        first = s * count - t0 * LANES
        for c in range(2):
            for d in range(2):
                w[c, first:first + count, d, :count] = forward[d * count:(d + 1) * count, c * count:(c + 1) * count].T
        cut.append(half(w.reshape(-1, 2 * LANES)))
    for t, (s0, s1) in enumerate(tiles):
        w = np.zeros((s1 - s0, 2, LANES, 2, LANES), np.float32)
        for s in range(s0, s1):
            for z in range(count):
                lane = s * count + z - t * LANES
                if 0 <= lane < LANES:
                    for c in range(2):
                        for d in range(2):
                            w[s - s0, c, :count, d, lane] = backward[d * count + z, c * count:(c + 1) * count]
        lay.append(half(w.reshape(-1, 2 * LANES)))
    return cut, lay


def piece_planes(count, ga, gb, device):
    rows = count // (ga * gb)
    ai, bi = divmod(device, gb)
    owners = [((ai + s) % ga) * gb + (bi + t) % gb for s in range(ga) for t in range(gb)]
    return np.concatenate([np.arange(o * rows, (o + 1) * rows) for o in owners])


def device_tables(count, ga, gb):
    forward, backward = complex_tables(count)
    near = count // ga
    fwd, bwd, mirror = [], [], []
    for device in range(ga * gb):
        planes = piece_planes(count, ga, gb, device)
        fwd.append(np.concatenate([forward[:, planes], forward[:, count + planes]], axis=1))
        bwd.append(np.concatenate([backward[planes[:near]], backward[count + planes[:near]]], axis=0))
        place = np.eye(count, dtype=np.float32)[:, planes]
        flip = place[(-np.arange(count)) % count]
        mirror.append(np.concatenate([place, flip], axis=1))
    return half(np.stack(fwd)), half(np.stack(bwd)), half(np.stack(mirror))


def line_selectors(count):
    lines, _ = line_spans(count)
    picks = []
    for s, (t0, t1) in enumerate(lines):
        w = np.zeros(((t1 - t0) * LANES, 2, LANES), np.float32)
        for z in range(count):
            w[s * count + z - t0 * LANES, 0, z] = 1
            w[s * count + z - t0 * LANES, 1, (-z) % count] = 1
        picks.append(half(w.reshape(-1, 2 * LANES)))
    return picks


def kernel_body(count, n, place_ref, *refs):
    pieces, mirror = refs[:n], refs[n]
    lines, _ = line_spans(count)
    picks = refs[n + 1:n + 1 + len(lines)]
    out_ref, cut_ref = refs[n + 1 + len(lines):]
    per = len(lines)
    width = TILES * LANES
    unrolled = 6

    def cut(step, carry):
        for u in range(unrolled):
            group = step * unrolled + u
            lanes = pl.ds(pl.multiple_of(group * width, LANES), width)
            k = jnp.concatenate([r[:, lanes].astype(F32) for r in pieces], axis=0).astype(BF)
            for s, (t0, t1) in enumerate(lines):
                cut_ref[group * per + s] = dot(k[:, t0 * LANES:t1 * LANES], picks[s][...]).astype(BF)
        return carry

    lax.fori_loop(0, count // (per * unrolled), cut, 0)

    def join(step, carry):
        for u in range(0, 16, 2):
            both = []
            for e in range(2):
                gx = step * 16 + u + e
                back = lax.rem(count - gx, count)
                both.append(jnp.concatenate([cut_ref[gx][:, :LANES], cut_ref[back][:, LANES:]], axis=0))
            value = dot(mirror[place_ref[0]], jnp.concatenate(both, axis=1)) * (0.5 / count**3)
            for e in range(2):
                out_ref[step * 16 + u + e] = value[:, e * LANES:(e + 1) * LANES]
        return carry

    lax.fori_loop(0, count // 16, join, 0)


def whole_kernel(pieces, place, mirror, count):
    picks = line_selectors(count)
    vmem = pl.BlockSpec(memory_space=pltpu.VMEM)
    ins = [*pieces, mirror, *picks]
    return pl.pallas_call(
        functools.partial(kernel_body, count, len(pieces)),
        out_shape=jax.ShapeDtypeStruct((count, count, LANES), F32),
        in_specs=[pl.BlockSpec(memory_space=pltpu.SMEM)] + [vmem] * len(ins),
        out_specs=vmem,
        scratch_shapes=[pltpu.VMEM((count, count, 2 * LANES), BF)],
        compiler_params=pltpu.CompilerParams(vmem_limit_bytes=VMEM_BYTES),
        cost_estimate=pl.CostEstimate(flops=FLOPS, bytes_accessed=10**3, transcendentals=0),
        name="symmetric_kernel",
    )(place, *ins)


def unit_body(count, n, near, a_count, b_count, places, kept_held, place_ref, *refs):
    refs = list(refs)

    def take(k):
        return [refs.pop(0) for _ in range(k)]

    lines, tiles = line_spans(count)
    per = len(lines)
    width = TILES * LANES
    pieces = take((a_count + b_count) * n)
    kern, x_tables, y_tables, z_tables_ref = take(4)
    kept_in = [take(near) for _ in range(a_count)] if kept_held else None
    sent_out, kept_out = take(b_count * near), take(a_count * near)
    held, k_ref, x_ref, y_ref, z_ref, sent_near, sent_rest, kept_ref, s_ref, r_ref = take(10)
    in_sem, table_sem, kept_sem, sent_sem, out_sem = take(5)
    rows = pieces[0].shape[1]
    core = lax.rem(place_ref[0], near)
    where = [core * step + offset if step else offset for step, offset in places]
    pitch = count + PITCH
    planes = near * rows
    steps = count // (per * GROUPS)
    chunk = count * count // CHUNKS
    pairs = [(i, j) for i in range(a_count) for j in range(b_count)]

    def lanes_of(part):
        return slice(part * chunk, (part + 1) * chunk)

    def piece_in(step, p):
        return pltpu.make_async_copy(
            pieces[p].at[where[p], :, lanes_of(step)], held.at[p, :, lanes_of(step)], in_sem.at[step, p]
        )

    def outgoing(step):
        lanes = lanes_of(step)
        copies = []
        for j in range(b_count):
            for p in range(near):
                source = sent_rest.at[j, p - 1, :, lanes] if p else sent_near.at[j, :, lanes]
                copies.append(
                    pltpu.make_async_copy(source, sent_out[j * near + p].at[:, lanes], sent_sem.at[step, j * near + p])
                )
        for i in range(a_count):
            for p in range(near):
                copies.append(
                    pltpu.make_async_copy(
                        kept_ref.at[i, p, :, lanes], kept_out[i * near + p].at[:, lanes], out_sem.at[step, i * near + p]
                    )
                )
        return copies

    cut_rows = sum(2 * (t1 - t0) * LANES for t0, t1 in lines)
    small = [
        pltpu.make_async_copy(z_tables_ref.at[:cut_rows], z_ref.at[:cut_rows], table_sem.at[0]),
        pltpu.make_async_copy(x_tables.at[place_ref[0]], x_ref, table_sem.at[1]),
        pltpu.make_async_copy(y_tables, y_ref, table_sem.at[2]),
    ]
    k_copy = pltpu.make_async_copy(kern, k_ref, table_sem.at[3])
    lay_copy = pltpu.make_async_copy(z_tables_ref.at[cut_rows:], z_ref.at[cut_rows:], table_sem.at[4])
    kept_copies = []
    if kept_held:
        for i in range(a_count):
            for p in range(near):
                kept_copies.append(
                    pltpu.make_async_copy(kept_in[i][p], kept_ref.at[i, p], kept_sem.at[i * near + p])
                )

    small[0].start()
    small[1].start()

    for part in range(CHUNKS):
        for p in range(len(pieces)):
            piece_in(part, p).start()
    small[2].start()
    k_copy.start()
    lay_copy.start()
    for copy in kept_copies:
        copy.start()

    spans_cut, spans_lay, at = [], [], 0
    for t0, t1 in lines:
        spans_cut.append(slice(at, at + 2 * (t1 - t0) * LANES))
        at += 2 * (t1 - t0) * LANES
    for s0, s1 in tiles:
        spans_lay.append(slice(at, at + 2 * (s1 - s0) * LANES))
        at += 2 * (s1 - s0) * LANES

    def stack(first, number, lanes):
        return jnp.concatenate([held[first + p, :, lanes].astype(F32) for p in range(number)], axis=0)

    small[0].wait()
    small[1].wait()

    def forward(step, carry):
        for part in range(CHUNKS):

            @pl.when(step == part * steps // CHUNKS)
            def _():
                for p in range(len(pieces)):
                    piece_in(part, p).wait()

        rho = [[], []]
        for g in range(GROUPS):
            lanes = pl.ds(pl.multiple_of((step * GROUPS + g) * width, LANES), width)
            a = [stack(i * n, n, lanes) for i in range(a_count)]
            b = [stack((a_count + j) * n, n, lanes) for j in range(b_count)]
            for k, (i, j) in enumerate(pairs):
                rho[k].append((a[i] * b[j]).astype(BF))
        rho = [jnp.concatenate(r, axis=0) for r in rho]
        along = []
        for s, (t0, t1) in enumerate(lines):
            lhs = jnp.concatenate([r[:, t0 * LANES:t1 * LANES] for r in rho], axis=1)
            along.append(dot(lhs, z_ref[spans_cut[s], :]).astype(BF))
        for g in range(GROUPS):
            parts = []
            for s in range(per):
                w = along[s][g * count:(g + 1) * count]
                parts.append(jnp.concatenate([w[:, :LANES], w[:, LANES:]], axis=0))
            out = dot(x_ref[:2 * count], jnp.concatenate(parts, axis=1))
            y = (step * GROUPS + g) * per
            for s in range(per):
                s_ref[pl.ds(y + s, 2 * count, pitch), :] = out[:, s * LANES:(s + 1) * LANES]
        return carry

    lax.fori_loop(0, steps, forward, 0)
    small[2].wait()
    k_copy.wait()

    def plane_set(ref, first):
        return jnp.concatenate(
            [
                jnp.concatenate(
                    [ref[pl.ds((c * count + first + e) * pitch, count), :].astype(BF) for c in range(2)], axis=0
                )
                for e in range(per)
            ],
            axis=1,
        )

    def middle(step, carry):
        firsts = [(step * UNROLL + u) * per for u in range(UNROLL)]
        summed = [dot(y_ref[:2 * count], plane_set(s_ref, gx)) for gx in firsts]
        spectra = []
        for gx, value in zip(firsts, summed):
            scale = jnp.concatenate([k_ref[gx + e] for e in range(per)], axis=1)
            spectra.append(
                jnp.concatenate([(value[:count] * scale).astype(BF), (value[count:] * scale).astype(BF)], axis=0)
            )
        backs = [dot(y_ref[2 * count:], spectrum) for spectrum in spectra]
        for gx, value in zip(firsts, backs):
            for e in range(per):
                r_ref[pl.ds(gx + e, 2 * count, pitch), :] = value[:, e * LANES:(e + 1) * LANES]
        return carry

    lax.fori_loop(0, count // (per * UNROLL), middle, 0)
    lay_copy.wait()
    for copy in kept_copies:
        copy.wait()

    def backward(step, carry):
        columns = []
        for g in range(GROUPS):
            out = dot(x_ref[2 * count:], plane_set(r_ref, (step * GROUPS + g) * per)).astype(BF)
            row = []
            for s in range(per):
                w = out[:, s * LANES:(s + 1) * LANES]
                row.append(jnp.concatenate([w[:planes], w[planes:]], axis=1))
            columns.append(row)
        for t, (s0, s1) in enumerate(tiles):
            lhs = jnp.concatenate([jnp.concatenate(row[s0:s1], axis=1) for row in columns], axis=0)
            potential = dot(lhs, z_ref[spans_lay[t], :])
            for g in range(GROUPS):
                lanes = pl.ds(pl.multiple_of((step * GROUPS + g) * width + t * LANES, LANES), LANES)
                minus = -potential[g * planes:(g + 1) * planes]
                a = [stack(i * n, near, lanes) for i in range(a_count)]
                b = [stack((a_count + j) * n, near, lanes) for j in range(b_count)]
                sent, kept = [None] * b_count, [None] * a_count
                for k, (i, j) in enumerate(pairs):
                    v = minus[:, k * LANES:(k + 1) * LANES]
                    sent[j] = v * a[i] if sent[j] is None else sent[j] + v * a[i]
                    kept[i] = v * b[j] if kept[i] is None else kept[i] + v * b[j]
                for p in range(near):
                    part = slice(p * rows, (p + 1) * rows)
                    for j in range(b_count):
                        if p:
                            sent_rest[j, p - 1, :, lanes] = sent[j][part].astype(sent_rest.dtype)
                        else:
                            sent_near[j, :, lanes] = sent[j][part]
                    for i in range(a_count):
                        value = kept[i][part]
                        if kept_held:
                            value = value + kept_ref[i, p, :, lanes]
                        kept_ref[i, p, :, lanes] = value
        for part in range(CHUNKS):

            @pl.when(step == (part + 1) * steps // CHUNKS - 1)
            def _():
                for copy in outgoing(part):
                    copy.start()

        return carry

    lax.fori_loop(0, steps, backward, 0)

    for part in range(CHUNKS):
        for copy in outgoing(part):
            copy.wait()


def unit(a, b, place, kern, x_tables, near, kept_in):
    count = kern.shape[0]
    n = len(a[0])
    rows, width = a[0][0][0].shape[1:]
    a_count, b_count = len(a), len(b)
    y_tables = np.concatenate([half(t) for t in complex_tables(count)], axis=0)
    cut, lay = z_tables(count)
    z_all = np.concatenate([*cut, *lay], axis=0)
    chosen = [r for pieces in (*a, *b) for r in pieces]
    ins = [r[0] for r in chosen] + [kern, x_tables, y_tables, z_all]
    if kept_in is not None:
        ins += [k for pieces in kept_in for k in pieces]
    anywhere = pl.BlockSpec(memory_space=pltpu.HBM)
    pieces = (a_count + b_count) * n
    outs = pl.pallas_call(
        functools.partial(
            unit_body, count, n, near, a_count, b_count, [r[1:] for r in chosen], kept_in is not None
        ),
        out_shape=[
            jax.ShapeDtypeStruct((rows, width), BF if p else F32) for _ in range(b_count) for p in range(near)
        ]
        + [jax.ShapeDtypeStruct((rows, width), F32)] * (a_count * near),
        in_specs=[pl.BlockSpec(memory_space=pltpu.SMEM)] + [anywhere] * len(ins),
        out_specs=[anywhere] * ((a_count + b_count) * near),
        scratch_shapes=[
            pltpu.VMEM((pieces, rows, width), BF),
            pltpu.VMEM(kern.shape, F32),
            pltpu.VMEM(x_tables.shape[1:], BF),
            pltpu.VMEM(y_tables.shape, BF),
            pltpu.VMEM(z_all.shape, BF),
            pltpu.VMEM((b_count, rows, width), F32),
            pltpu.VMEM((b_count, near - 1, rows, width), BF),
            pltpu.VMEM((a_count, near, rows, width), F32),
            pltpu.VMEM((2 * count * (count + PITCH), LANES), F32),
            pltpu.VMEM((2 * count * (count + PITCH), LANES), F32),
            pltpu.SemaphoreType.DMA((CHUNKS, pieces)),
            pltpu.SemaphoreType.DMA((5,)),
            pltpu.SemaphoreType.DMA((a_count * near,)),
            pltpu.SemaphoreType.DMA((CHUNKS, b_count * near)),
            pltpu.SemaphoreType.DMA((CHUNKS, a_count * near)),
        ],
        compiler_params=pltpu.CompilerParams(vmem_limit_bytes=VMEM_BYTES),
        cost_estimate=pl.CostEstimate(flops=FLOPS, bytes_accessed=10**3, transcendentals=0),
        name="pair_potentials",
    )(place, *ins)
    sent = [outs[j * near:(j + 1) * near] for j in range(b_count)]
    kept = [outs[(b_count + i) * near:(b_count + i + 1) * near] for i in range(a_count)]
    return sent, kept


def split_of(n):
    gb = 1
    while gb * gb < n and gb < 4:
        gb *= 2
    return n // gb, gb


def after(value, *events):
    return lax.optimization_barrier((value, *events))[0]


def local(orbitals, kernel, *, ga, gb):
    band_count, rows, width = orbitals.shape
    n = ga * gb
    count = rows * n
    na = band_count // gb
    blocks = lax.axis_size("band")
    me = lax.axis_index("grid")
    bi = me % gb

    def hop(x, distance):
        return lax.ppermute(x, "band", [(i, (i + distance) % blocks) for i in range(blocks)])

    def to_a(x, s):
        return lax.ppermute(x, "grid", [(((i // gb + s) % ga) * gb + i % gb, i) for i in range(n)])

    def to_b(x, t):
        return lax.ppermute(x, "grid", [((i // gb) * gb + (i % gb + t) % gb, i) for i in range(n)])

    order = [(s, t) for s in range(ga) for t in range(gb)]
    fwd, bwd, mirror = device_tables(count, ga, gb)
    x_tables = jnp.asarray(np.concatenate([fwd, bwd], axis=1))

    place = me.astype(jnp.int32).reshape(1)

    def others(x):
        return [to_b(x, t) for t in range(1, gb)]

    own_near = [orbitals, *others(orbitals)]
    late = after(orbitals, own_near[1])
    rest = [late[gb + 1:]] if na > 1 else []
    first_near = late[:gb + 1] if na > 1 else orbitals
    k_own = kernel.astype(BF)
    k_near = [k_own, *others(k_own)]
    k_far = [to_a(k_own, s) for s in range(1, ga)]
    block = hop(first_near, DIST)
    first_own = [to_a(orbitals[:gb], s) for s in range(1, ga)]
    first_own, rest, own_near, k_far = lax.optimization_barrier((first_own, rest, own_near, k_far))
    shares = [after(orbitals, *first_own)[index * gb:(index + 1) * gb] if index else None for index in range(na)]
    if na > 1:
        k_far = [after(r, *shares[1:]) for r in k_far]

    k_rows = list(k_near)
    for r in k_far:
        k_rows += [r, *others(r)]
    kern = whole_kernel(k_rows, place, after(jnp.asarray(mirror), block), count)
    near_blocks = [[x, *others(x)] for x in [block]]
    far_pieces = [[[r, *others(r)] for r in first_own]]
    forwarded = [hop(r, DIST) for r in first_own]
    later_far = [[to_a(shares[index], s) for s in range(1, ga)] for index in range(1, na)]
    later_far, forwarded, kern, rest = lax.optimization_barrier((later_far, forwarded, kern, rest))
    far_pieces += [[[r, *others(r)] for r in far] for far in later_far]
    first_far = [[r, *others(r)] for r in forwarded]
    landed = [hop(x, DIST) for x in rest]

    own = []
    for index in range(na):
        pieces = [(r, 1, index * gb) for r in own_near]
        pieces += [(r, 1, 0) for group in far_pieces[index] for r in group]
        own.append(pieces)
    near = [[(r, 0, j) for r in near_blocks[0]] for j in range(first_near.shape[0])]

    def partner(j, *events):
        if j < gb:
            return near[j] + [(x, 0, j) for group in first_far for x in group]
        pieces = list(near[j]) if j < len(near) else [(r, 0, 0) for r in [landed[0], *others(landed[0])]]
        for s in range(1, ga):
            x = to_a(singles[j], s)
            x = after(x, sent_by[j - gb])
            pieces += [(y, 0, 0) for y in [x, *others(x)]]
        return pieces

    returned = [None] * band_count
    events = []

    def send_back(sent, j):
        if j == band_count - 1 and per_unit == 1:
            sent = [sent[0], *(after(x, returned[j - 2]) for x in sent[1:])]
        total = sent[0]
        for t in range(1, gb):
            total = total + to_b(sent[t], gb - t).astype(F32)
        total = total.astype(BF)
        events.append(total)
        returned[j] = hop(total, -DIST)

    per_unit = 2 // na
    kept = None
    sent_by = []
    one = lax.optimization_barrier(jnp.ones((), BF))
    singles = {}
    for u in range(0, band_count, per_unit):
        b = [partner(j) for j in range(u, u + per_unit)]
        waits = []
        if u > 1 and per_unit == 1:
            waits = [*events[max(u - 2, 0):u if u == band_count - 1 else u - 1], *returned[:u - 2]]
        if na > 1 and u < 2:
            if u:
                landed[0] = after(landed[0], sent_by[-1])
            singles[gb + u] = landed[0] * one if u else after(block, later_far)[gb:gb + 1]
            waits = [*waits, singles[gb + u]]
        tables = after(x_tables, *waits) if waits else x_tables
        sent, kept = unit(own, b, place, kern, tables, gb, kept)
        sent_by.append(sent[0][0])
        for e in range(per_unit):
            send_back(sent[e], u + e)

    parts = [[x[0] for x in kept]]
    for t in range(1, gb):
        received = to_b(jnp.stack([x[t] for x in kept]).astype(BF), gb - t)
        parts.append([received[index].astype(F32) for index in range(na)])
    rows_out = []
    for j in range(band_count):
        index, owner = divmod(j, gb)
        which = (bi - owner + gb) % gb
        value = parts[0][index]
        for t in range(1, gb):
            value = jnp.where(which == t, parts[t][index], value)
        rows_out.append(value)
    early = band_count - per_unit
    base = lax.optimization_barrier(
        jnp.stack([v + returned[j].astype(F32) if j < early else v for j, v in enumerate(rows_out)])
    )
    last = base[early:] + jnp.stack(returned[early:]).astype(F32)
    return lax.dynamic_update_slice(base, last, (early, 0, 0))


def solution(mesh):
    ga, gb = split_of(mesh.shape["grid"])
    placed = (P("band", "grid", None), P("grid", None))
    return jax.shard_map(
        functools.partial(local, ga=ga, gb=gb),
        mesh=mesh,
        in_specs=placed,
        out_specs=P("band", "grid", None),
        check_vma=False,
    )
```

```python
import functools

import jax
import jax.numpy as jnp
import ml_dtypes
import numpy as np
from jax import lax
from jax.experimental import pallas as pl
from jax.experimental.pallas import tpu as pltpu
from jax.sharding import PartitionSpec as P

DIST = 1
LANES = 128
TILES = 3
GROUPS = 12
UNROLL = 24
CHUNKS = 2
PITCH = 4
BF = jnp.bfloat16
F32 = jnp.float32
FLOPS = 10**11
VMEM_BYTES = 62 * 1024 * 1024


def dot(a, b):
    return jnp.dot(a, b, preferred_element_type=F32)


def half(a):
    return np.asarray(a, np.float32).astype(ml_dtypes.bfloat16)


def complex_tables(count):
    j = np.arange(count)
    angles = (j[:, None] * j[None, :] % count).astype(np.float32) * np.float32(2.0 * np.pi / count)
    cosine = half(np.cos(angles)).astype(np.float32)
    sine = half(np.sin(angles)).astype(np.float32)
    forward = np.block([[cosine, sine], [-sine, cosine]])
    backward = np.block([[cosine, -sine], [sine, cosine]])
    return forward, backward


def line_spans(count):
    per = TILES * LANES // count
    lines = [(s * count // LANES, -(-(s + 1) * count // LANES)) for s in range(per)]
    tiles = [(t * LANES // count, -(-(t + 1) * LANES // count)) for t in range(TILES)]
    return lines, tiles


def z_tables(count):
    forward, backward = complex_tables(count)
    lines, tiles = line_spans(count)
    cut, lay = [], []
    for s, (t0, t1) in enumerate(lines):
        w = np.zeros((2, (t1 - t0) * LANES, 2, LANES), np.float32)
        first = s * count - t0 * LANES
        for c in range(2):
            for d in range(2):
                w[c, first:first + count, d, :count] = forward[d * count:(d + 1) * count, c * count:(c + 1) * count].T
        cut.append(half(w.reshape(-1, 2 * LANES)))
    for t, (s0, s1) in enumerate(tiles):
        w = np.zeros((s1 - s0, 2, LANES, 2, LANES), np.float32)
        for s in range(s0, s1):
            for z in range(count):
                lane = s * count + z - t * LANES
                if 0 <= lane < LANES:
                    for c in range(2):
                        for d in range(2):
                            w[s - s0, c, :count, d, lane] = backward[d * count + z, c * count:(c + 1) * count]
        lay.append(half(w.reshape(-1, 2 * LANES)))
    return cut, lay


def piece_planes(count, ga, gb, device):
    rows = count // (ga * gb)
    ai, bi = divmod(device, gb)
    owners = [((ai + s) % ga) * gb + (bi + t) % gb for s in range(ga) for t in range(gb)]
    return np.concatenate([np.arange(o * rows, (o + 1) * rows) for o in owners])


def device_tables(count, ga, gb):
    forward, backward = complex_tables(count)
    near = count // ga
    fwd, bwd, mirror = [], [], []
    for device in range(ga * gb):
        planes = piece_planes(count, ga, gb, device)
        fwd.append(np.concatenate([forward[:, planes], forward[:, count + planes]], axis=1))
        bwd.append(np.concatenate([backward[planes[:near]], backward[count + planes[:near]]], axis=0))
        place = np.eye(count, dtype=np.float32)[:, planes]
        flip = place[(-np.arange(count)) % count]
        mirror.append(np.concatenate([place, flip], axis=1))
    return half(np.stack(fwd)), half(np.stack(bwd)), half(np.stack(mirror))


def line_selectors(count):
    lines, _ = line_spans(count)
    picks = []
    for s, (t0, t1) in enumerate(lines):
        w = np.zeros(((t1 - t0) * LANES, 2, LANES), np.float32)
        for z in range(count):
            w[s * count + z - t0 * LANES, 0, z] = 1
            w[s * count + z - t0 * LANES, 1, (-z) % count] = 1
        picks.append(half(w.reshape(-1, 2 * LANES)))
    return picks


def kernel_body(count, n, place_ref, *refs):
    pieces, mirror = refs[:n], refs[n]
    lines, _ = line_spans(count)
    picks = refs[n + 1:n + 1 + len(lines)]
    out_ref, cut_ref = refs[n + 1 + len(lines):]
    per = len(lines)
    width = TILES * LANES
    unrolled = 6

    def cut(step, carry):
        for u in range(unrolled):
            group = step * unrolled + u
            lanes = pl.ds(pl.multiple_of(group * width, LANES), width)
            k = jnp.concatenate([r[:, lanes].astype(F32) for r in pieces], axis=0).astype(BF)
            for s, (t0, t1) in enumerate(lines):
                cut_ref[group * per + s] = dot(k[:, t0 * LANES:t1 * LANES], picks[s][...]).astype(BF)
        return carry

    lax.fori_loop(0, count // (per * unrolled), cut, 0)

    def join(step, carry):
        for u in range(0, 16, 2):
            both = []
            for e in range(2):
                gx = step * 16 + u + e
                back = lax.rem(count - gx, count)
                both.append(jnp.concatenate([cut_ref[gx][:, :LANES], cut_ref[back][:, LANES:]], axis=0))
            value = dot(mirror[place_ref[0]], jnp.concatenate(both, axis=1)) * (0.5 / count**3)
            for e in range(2):
                out_ref[step * 16 + u + e] = value[:, e * LANES:(e + 1) * LANES]
        return carry

    lax.fori_loop(0, count // 16, join, 0)


def whole_kernel(pieces, place, mirror, count):
    picks = line_selectors(count)
    vmem = pl.BlockSpec(memory_space=pltpu.VMEM)
    ins = [*pieces, mirror, *picks]
    return pl.pallas_call(
        functools.partial(kernel_body, count, len(pieces)),
        out_shape=jax.ShapeDtypeStruct((count, count, LANES), F32),
        in_specs=[pl.BlockSpec(memory_space=pltpu.SMEM)] + [vmem] * len(ins),
        out_specs=vmem,
        scratch_shapes=[pltpu.VMEM((count, count, 2 * LANES), BF)],
        compiler_params=pltpu.CompilerParams(vmem_limit_bytes=VMEM_BYTES),
        cost_estimate=pl.CostEstimate(flops=FLOPS, bytes_accessed=10**3, transcendentals=0),
        name="symmetric_kernel",
    )(place, *ins)


def unit_body(count, n, near, a_count, b_count, places, kept_held, place_ref, *refs):
    refs = list(refs)

    def take(k):
        return [refs.pop(0) for _ in range(k)]

    lines, tiles = line_spans(count)
    per = len(lines)
    width = TILES * LANES
    pieces = take((a_count + b_count) * n)
    kern, x_tables, y_tables, z_tables_ref = take(4)
    kept_in = [take(near) for _ in range(a_count)] if kept_held else None
    sent_out, kept_out = take(b_count * near), take(a_count * near)
    held, k_ref, x_ref, y_ref, z_ref, sent_near, sent_rest, kept_ref, s_ref, r_ref = take(10)
    in_sem, table_sem, kept_sem, sent_sem, out_sem = take(5)
    rows = pieces[0].shape[1]
    core = lax.rem(place_ref[0], near)
    where = [core * step + offset if step else offset for step, offset in places]
    pitch = count + PITCH
    planes = near * rows
    steps = count // (per * GROUPS)
    chunk = count * count // CHUNKS
    pairs = [(i, j) for i in range(a_count) for j in range(b_count)]

    def lanes_of(part):
        return slice(part * chunk, (part + 1) * chunk)

    def piece_in(step, p):
        return pltpu.make_async_copy(
            pieces[p].at[where[p], :, lanes_of(step)], held.at[p, :, lanes_of(step)], in_sem.at[step, p]
        )

    def outgoing(step):
        lanes = lanes_of(step)
        copies = []
        for j in range(b_count):
            for p in range(near):
                source = sent_rest.at[j, p - 1, :, lanes] if p else sent_near.at[j, :, lanes]
                copies.append(
                    pltpu.make_async_copy(source, sent_out[j * near + p].at[:, lanes], sent_sem.at[step, j * near + p])
                )
        for i in range(a_count):
            for p in range(near):
                copies.append(
                    pltpu.make_async_copy(
                        kept_ref.at[i, p, :, lanes], kept_out[i * near + p].at[:, lanes], out_sem.at[step, i * near + p]
                    )
                )
        return copies

    cut_rows = sum(2 * (t1 - t0) * LANES for t0, t1 in lines)
    small = [
        pltpu.make_async_copy(z_tables_ref.at[:cut_rows], z_ref.at[:cut_rows], table_sem.at[0]),
        pltpu.make_async_copy(x_tables.at[place_ref[0]], x_ref, table_sem.at[1]),
        pltpu.make_async_copy(y_tables, y_ref, table_sem.at[2]),
    ]
    k_copy = pltpu.make_async_copy(kern, k_ref, table_sem.at[3])
    lay_copy = pltpu.make_async_copy(z_tables_ref.at[cut_rows:], z_ref.at[cut_rows:], table_sem.at[4])
    kept_copies = []
    if kept_held:
        for i in range(a_count):
            for p in range(near):
                kept_copies.append(
                    pltpu.make_async_copy(kept_in[i][p], kept_ref.at[i, p], kept_sem.at[i * near + p])
                )

    small[0].start()
    small[1].start()

    for part in range(CHUNKS):
        for p in range(len(pieces)):
            piece_in(part, p).start()
    small[2].start()
    k_copy.start()
    lay_copy.start()
    for copy in kept_copies:
        copy.start()

    spans_cut, spans_lay, at = [], [], 0
    for t0, t1 in lines:
        spans_cut.append(slice(at, at + 2 * (t1 - t0) * LANES))
        at += 2 * (t1 - t0) * LANES
    for s0, s1 in tiles:
        spans_lay.append(slice(at, at + 2 * (s1 - s0) * LANES))
        at += 2 * (s1 - s0) * LANES

    def stack(first, number, lanes):
        return jnp.concatenate([held[first + p, :, lanes].astype(F32) for p in range(number)], axis=0)

    small[0].wait()
    small[1].wait()

    def forward(step, carry):
        for part in range(CHUNKS):

            @pl.when(step == part * steps // CHUNKS)
            def _():
                for p in range(len(pieces)):
                    piece_in(part, p).wait()

        rho = [[], []]
        for g in range(GROUPS):
            lanes = pl.ds(pl.multiple_of((step * GROUPS + g) * width, LANES), width)
            a = [stack(i * n, n, lanes) for i in range(a_count)]
            b = [stack((a_count + j) * n, n, lanes) for j in range(b_count)]
            for k, (i, j) in enumerate(pairs):
                rho[k].append((a[i] * b[j]).astype(BF))
        rho = [jnp.concatenate(r, axis=0) for r in rho]
        along = []
        for s, (t0, t1) in enumerate(lines):
            lhs = jnp.concatenate([r[:, t0 * LANES:t1 * LANES] for r in rho], axis=1)
            along.append(dot(lhs, z_ref[spans_cut[s], :]).astype(BF))
        for g in range(GROUPS):
            parts = []
            for s in range(per):
                w = along[s][g * count:(g + 1) * count]
                parts.append(jnp.concatenate([w[:, :LANES], w[:, LANES:]], axis=0))
            out = dot(x_ref[:2 * count], jnp.concatenate(parts, axis=1))
            y = (step * GROUPS + g) * per
            for s in range(per):
                s_ref[pl.ds(y + s, 2 * count, pitch), :] = out[:, s * LANES:(s + 1) * LANES]
        return carry

    lax.fori_loop(0, steps, forward, 0)
    small[2].wait()
    k_copy.wait()

    def plane_set(ref, first):
        return jnp.concatenate(
            [
                jnp.concatenate(
                    [ref[pl.ds((c * count + first + e) * pitch, count), :].astype(BF) for c in range(2)], axis=0
                )
                for e in range(per)
            ],
            axis=1,
        )

    def middle(step, carry):
        firsts = [(step * UNROLL + u) * per for u in range(UNROLL)]
        summed = [dot(y_ref[:2 * count], plane_set(s_ref, gx)) for gx in firsts]
        spectra = []
        for gx, value in zip(firsts, summed):
            scale = jnp.concatenate([k_ref[gx + e] for e in range(per)], axis=1)
            spectra.append(
                jnp.concatenate([(value[:count] * scale).astype(BF), (value[count:] * scale).astype(BF)], axis=0)
            )
        backs = [dot(y_ref[2 * count:], spectrum) for spectrum in spectra]
        for gx, value in zip(firsts, backs):
            for e in range(per):
                r_ref[pl.ds(gx + e, 2 * count, pitch), :] = value[:, e * LANES:(e + 1) * LANES]
        return carry

    lax.fori_loop(0, count // (per * UNROLL), middle, 0)
    lay_copy.wait()
    for copy in kept_copies:
        copy.wait()

    def backward(step, carry):
        columns = []
        for g in range(GROUPS):
            out = dot(x_ref[2 * count:], plane_set(r_ref, (step * GROUPS + g) * per)).astype(BF)
            row = []
            for s in range(per):
                w = out[:, s * LANES:(s + 1) * LANES]
                row.append(jnp.concatenate([w[:planes], w[planes:]], axis=1))
            columns.append(row)
        for t, (s0, s1) in enumerate(tiles):
            lhs = jnp.concatenate([jnp.concatenate(row[s0:s1], axis=1) for row in columns], axis=0)
            potential = dot(lhs, z_ref[spans_lay[t], :])
            for g in range(GROUPS):
                lanes = pl.ds(pl.multiple_of((step * GROUPS + g) * width + t * LANES, LANES), LANES)
                minus = -potential[g * planes:(g + 1) * planes]
                a = [stack(i * n, near, lanes) for i in range(a_count)]
                b = [stack((a_count + j) * n, near, lanes) for j in range(b_count)]
                sent, kept = [None] * b_count, [None] * a_count
                for k, (i, j) in enumerate(pairs):
                    v = minus[:, k * LANES:(k + 1) * LANES]
                    sent[j] = v * a[i] if sent[j] is None else sent[j] + v * a[i]
                    kept[i] = v * b[j] if kept[i] is None else kept[i] + v * b[j]
                for p in range(near):
                    part = slice(p * rows, (p + 1) * rows)
                    for j in range(b_count):
                        if p:
                            sent_rest[j, p - 1, :, lanes] = sent[j][part].astype(sent_rest.dtype)
                        else:
                            sent_near[j, :, lanes] = sent[j][part]
                    for i in range(a_count):
                        value = kept[i][part]
                        if kept_held:
                            value = value + kept_ref[i, p, :, lanes]
                        kept_ref[i, p, :, lanes] = value
        for part in range(CHUNKS):

            @pl.when(step == (part + 1) * steps // CHUNKS - 1)
            def _():
                for copy in outgoing(part):
                    copy.start()

        return carry

    lax.fori_loop(0, steps, backward, 0)

    for part in range(CHUNKS):
        for copy in outgoing(part):
            copy.wait()


def unit(a, b, place, kern, x_tables, near, kept_in):
    count = kern.shape[0]
    n = len(a[0])
    rows, width = a[0][0][0].shape[1:]
    a_count, b_count = len(a), len(b)
    y_tables = np.concatenate([half(t) for t in complex_tables(count)], axis=0)
    cut, lay = z_tables(count)
    z_all = np.concatenate([*cut, *lay], axis=0)
    chosen = [r for pieces in (*a, *b) for r in pieces]
    ins = [r[0] for r in chosen] + [kern, x_tables, y_tables, z_all]
    if kept_in is not None:
        ins += [k for pieces in kept_in for k in pieces]
    anywhere = pl.BlockSpec(memory_space=pltpu.HBM)
    pieces = (a_count + b_count) * n
    outs = pl.pallas_call(
        functools.partial(
            unit_body, count, n, near, a_count, b_count, [r[1:] for r in chosen], kept_in is not None
        ),
        out_shape=[
            jax.ShapeDtypeStruct((rows, width), BF if p else F32) for _ in range(b_count) for p in range(near)
        ]
        + [jax.ShapeDtypeStruct((rows, width), F32)] * (a_count * near),
        in_specs=[pl.BlockSpec(memory_space=pltpu.SMEM)] + [anywhere] * len(ins),
        out_specs=[anywhere] * ((a_count + b_count) * near),
        scratch_shapes=[
            pltpu.VMEM((pieces, rows, width), BF),
            pltpu.VMEM(kern.shape, F32),
            pltpu.VMEM(x_tables.shape[1:], BF),
            pltpu.VMEM(y_tables.shape, BF),
            pltpu.VMEM(z_all.shape, BF),
            pltpu.VMEM((b_count, rows, width), F32),
            pltpu.VMEM((b_count, near - 1, rows, width), BF),
            pltpu.VMEM((a_count, near, rows, width), F32),
            pltpu.VMEM(((2 * count + 1) * (count + PITCH), LANES), F32),
            pltpu.VMEM(((2 * count + 1) * (count + PITCH), LANES), F32),
            pltpu.SemaphoreType.DMA((CHUNKS, pieces)),
            pltpu.SemaphoreType.DMA((5,)),
            pltpu.SemaphoreType.DMA((a_count * near,)),
            pltpu.SemaphoreType.DMA((CHUNKS, b_count * near)),
            pltpu.SemaphoreType.DMA((CHUNKS, a_count * near)),
        ],
        compiler_params=pltpu.CompilerParams(vmem_limit_bytes=VMEM_BYTES),
        cost_estimate=pl.CostEstimate(flops=FLOPS, bytes_accessed=10**3, transcendentals=0),
        name="pair_potentials",
    )(place, *ins)
    sent = [outs[j * near:(j + 1) * near] for j in range(b_count)]
    kept = [outs[(b_count + i) * near:(b_count + i + 1) * near] for i in range(a_count)]
    return sent, kept


def split_of(n):
    gb = 1
    while gb * gb < n and gb < 4:
        gb *= 2
    return n // gb, gb


def after(value, *events):
    return lax.optimization_barrier((value, *events))[0]


def local(orbitals, kernel, *, ga, gb):
    band_count, rows, width = orbitals.shape
    n = ga * gb
    count = rows * n
    na = band_count // gb
    blocks = lax.axis_size("band")
    me = lax.axis_index("grid")
    bi = me % gb

    def hop(x, distance):
        return lax.ppermute(x, "band", [(i, (i + distance) % blocks) for i in range(blocks)])

    def to_a(x, s):
        return lax.ppermute(x, "grid", [(((i // gb + s) % ga) * gb + i % gb, i) for i in range(n)])

    def to_b(x, t):
        return lax.ppermute(x, "grid", [((i // gb) * gb + (i % gb + t) % gb, i) for i in range(n)])

    order = [(s, t) for s in range(ga) for t in range(gb)]
    fwd, bwd, mirror = device_tables(count, ga, gb)
    x_tables = jnp.asarray(np.concatenate([fwd, bwd], axis=1))

    place = me.astype(jnp.int32).reshape(1)

    def others(x):
        return [to_b(x, t) for t in range(1, gb)]

    own_near = [orbitals, *others(orbitals)]
    late = after(orbitals, own_near[1])
    rest = [late[gb + 1:]] if na > 1 else []
    first_near = late[:gb + 1] if na > 1 else orbitals
    k_own = kernel.astype(BF)
    k_near = [k_own, *others(k_own)]
    k_far = [to_a(k_own, s) for s in range(1, ga)]
    block = hop(first_near, DIST)
    first_own = [to_a(orbitals[:gb], s) for s in range(1, ga)]
    first_own, rest, own_near, k_far = lax.optimization_barrier((first_own, rest, own_near, k_far))
    shares = [after(orbitals, *first_own)[index * gb:(index + 1) * gb] if index else None for index in range(na)]
    if na > 1:
        k_far = [after(r, *shares[1:]) for r in k_far]

    k_rows = list(k_near)
    for r in k_far:
        k_rows += [r, *others(r)]
    kern = whole_kernel(k_rows, place, after(jnp.asarray(mirror), block), count)
    near_blocks = [[x, *others(x)] for x in [block]]
    far_pieces = [[[r, *others(r)] for r in first_own]]
    forwarded = [hop(r, DIST) for r in first_own]
    later_far = [[to_a(shares[index], s) for s in range(1, ga)] for index in range(1, na)]
    later_far, forwarded, kern, rest = lax.optimization_barrier((later_far, forwarded, kern, rest))
    far_pieces += [[[r, *others(r)] for r in far] for far in later_far]
    first_far = [[r, *others(r)] for r in forwarded]
    landed = [hop(x, DIST) for x in rest]

    own = []
    for index in range(na):
        pieces = [(r, 1, index * gb) for r in own_near]
        pieces += [(r, 1, 0) for group in far_pieces[index] for r in group]
        own.append(pieces)
    near = [[(r, 0, j) for r in near_blocks[0]] for j in range(first_near.shape[0])]

    def partner(j, *events):
        if j < gb:
            return near[j] + [(x, 0, j) for group in first_far for x in group]
        pieces = list(near[j]) if j < len(near) else [(r, 0, 0) for r in [landed[0], *others(landed[0])]]
        for s in range(1, ga):
            x = to_a(singles[j], s)
            x = after(x, sent_by[j - gb])
            pieces += [(y, 0, 0) for y in [x, *others(x)]]
        return pieces

    returned = [None] * band_count
    events = []

    def send_back(sent, j):
        if j == band_count - 1 and per_unit == 1:
            sent = [sent[0], *(after(x, returned[j - 2]) for x in sent[1:])]
        total = sent[0]
        for t in range(1, gb):
            total = total + to_b(sent[t], gb - t).astype(F32)
        total = total.astype(BF)
        events.append(total)
        returned[j] = hop(total, -DIST)

    per_unit = 2 // na
    kept = None
    sent_by = []
    one = lax.optimization_barrier(jnp.ones((), BF))
    singles = {}
    for u in range(0, band_count, per_unit):
        b = [partner(j) for j in range(u, u + per_unit)]
        waits = []
        if u > 1 and per_unit == 1:
            waits = [*events[max(u - 2, 0):u if u == band_count - 1 else u - 1], *returned[:u - 2]]
        if na > 1 and u < 2:
            if u:
                landed[0] = after(landed[0], sent_by[-1])
            singles[gb + u] = landed[0] * one if u else after(block, later_far)[gb:gb + 1]
            waits = [*waits, singles[gb + u]]
        tables = after(x_tables, *waits) if waits else x_tables
        sent, kept = unit(own, b, place, kern, tables, gb, kept)
        sent_by.append(sent[0][0])
        for e in range(per_unit):
            send_back(sent[e], u + e)

    parts = [[x[0] for x in kept]]
    for t in range(1, gb):
        received = to_b(jnp.stack([x[t] for x in kept]).astype(BF), gb - t)
        parts.append([received[index].astype(F32) for index in range(na)])
    rows_out = []
    for j in range(band_count):
        index, owner = divmod(j, gb)
        which = (bi - owner + gb) % gb
        value = parts[0][index]
        for t in range(1, gb):
            value = jnp.where(which == t, parts[t][index], value)
        rows_out.append(value)
    early = band_count - per_unit
    base = lax.optimization_barrier(
        jnp.stack([v + returned[j].astype(F32) if j < early else v for j, v in enumerate(rows_out)])
    )
    last = base[early:] + jnp.stack(returned[early:]).astype(F32)
    return lax.dynamic_update_slice(base, last, (early, 0, 0))


def solution(mesh):
    ga, gb = split_of(mesh.shape["grid"])
    placed = (P("band", "grid", None), P("grid", None))
    return jax.shard_map(
        functools.partial(local, ga=ga, gb=gb),
        mesh=mesh,
        in_specs=placed,
        out_specs=P("band", "grid", None),
        check_vma=False,
    )
```
